256 devices in a mesh: tm: 16 (over y, x_hi, core), space: 16 (over x_lo, z).
Axes of the slice: x: 4 (x_hi: 2, x_lo: 2; x = x_hi * 2 + x_lo), y: 4, z: 8, core: 2. Of those that a mesh axis runs over, the one named last changes fastest.
Arguments:
- adjoint_iterate: float32 [128, 16, 128, 128], P('tm', None, 'space'), may hold values from -6 to 6
- innovations: float32 [128, 16, 2048], P('tm', None, 'space'), may hold values from -6 to 6
- station_cells: int32 [128, 2048], P('tm', 'space'), may hold values from 0 to 1023
- diffusivity: float32 [16, 128, 128], P(None, 'space'), may hold values from 0.01 to 0.08
- wind_x: float32 [16, 128, 128], P(None, 'space'), may hold values from -0.2 to 0.2
- wind_y: float32 [16, 128, 128], P(None, 'space'), may hold values from -0.2 to 0.2
- vertical_mixing: float32 [16, 128, 128], P(None, 'space'), may hold values from 0.01 to 0.1
Outputs:
- updated_iterate: float32 [128, 16, 128, 128], P('tm', None, 'space')
The draws below stay inside these ranges and needn't reach their ends.
Inputs may be any that keep to these rules, and one draw needn't show every extreme that they name: `station_cells`: A station's column within its tile of 8 x 128 columns is numbered x * 128 + y; several stations may share a column.
All inputs are finite; a program needn't handle non-finite values.
Results may differ from the reference program's by a relative error of at most 0.0003.
Values sent between devices are 32-bit elements; how exact they have to be, the bound alone decides.
A program may use at most 64 MiB of HBM per device.

```python
import math
import jax
import jax.numpy as jnp

LEV = 16
TX = 8
NY = 128
STATIONS = 128
INNER = 4
NX = 128
STEPS = 128
STATIONS_ALL = 2048


def with_ends(drawn, stream_key, least, largest):
    place = [jax.random.randint(jax.random.fold_in(stream_key, axis), (), 0, length) for axis, length in enumerate(drawn.shape)]
    widest = drawn.shape.index(max(drawn.shape))
    next_to = place[:widest] + [(place[widest] + 1) % drawn.shape[widest]] + place[widest + 1:]
    return drawn.at[tuple(place)].set(least).at[tuple(next_to)].set(largest)


def block_scale(key, extent, shards, least, high):
    factor_of, own = 1.0, jax.random.fold_in(key, 6)
    for axis_at, parts in shards:
        steps = jnp.exp(jax.random.uniform(jax.random.fold_in(own, axis_at), (parts,), jnp.float32, least / len(shards), high / len(shards)))
        factor_of = factor_of * jnp.repeat(steps, extent[axis_at] // parts).reshape([-1 if axis == axis_at else 1 for axis in range(len(extent))])
    return factor_of


def scatter_about(rng, shape, width, reach, split=(), held_as=jnp.bfloat16):
    drawn = width * jax.random.normal(rng, shape, jnp.float32)
    if split:
        drawn = drawn * block_scale(rng, shape, split, -0.22, 0.18)
    return jnp.clip(drawn, -reach, reach).astype(held_as)


def setup_inputs(seed: int = 0) -> dict:
    key_list = jax.random.split(jax.random.key(seed), 8)
    return {
        "adjoint_iterate": scatter_about(key_list[0], (STEPS, LEV, NX, NY), 1.0, 6.0, ((0, 16), (2, 16)), jnp.float32),
        "innovations": scatter_about(key_list[1], (STEPS, LEV, STATIONS_ALL), 1.0, 6.0, ((0, 16), (2, 16)), jnp.float32),
        "station_cells": with_ends(jax.random.randint(key_list[2], (STEPS, STATIONS_ALL), 0, TX * NY), jax.random.fold_in(key_list[2], 1), 0, (TX * NY) - 1).astype(jnp.int32),
        "diffusivity": jnp.clip(jnp.exp(math.log(0.08) - 2.0794415 * jax.random.uniform(key_list[3], (LEV, NX, NY), jnp.float32) ** block_scale(key_list[3], (LEV, NX, NY), ((1, 16),), -0.2, 0.2)), 0.01, 0.08),
        "wind_x": jnp.clip(jax.random.uniform(key_list[4], (LEV, NX, NY), jnp.float32, -0.2, 0.2) * block_scale(key_list[4], (LEV, NX, NY), ((1, 16),), -0.4, 0.0), -0.2, 0.2),
        "wind_y": jnp.clip(jax.random.uniform(key_list[5], (LEV, NX, NY), jnp.float32, -0.2, 0.2) * block_scale(key_list[5], (LEV, NX, NY), ((1, 16),), -0.4, 0.0), -0.2, 0.2),
        "vertical_mixing": jnp.clip(jnp.exp(math.log(0.1) - 2.3025851 * jax.random.uniform(key_list[6], (LEV, NX, NY), jnp.float32) ** block_scale(key_list[6], (LEV, NX, NY), ((1, 16),), -0.2, 0.2)), 0.01, 0.1),
    }


circ_alpha = 0.1


def transfer_rates(diffusivity, wind_x, wind_y, vertical_mixing):
    east_rate = diffusivity + jnp.maximum(-wind_x, 0.0)
    west_rate = diffusivity + jnp.maximum(wind_x, 0.0)
    north_rate = diffusivity + jnp.maximum(-wind_y, 0.0)
    south_rate = diffusivity + jnp.maximum(wind_y, 0.0)
    return jnp.stack([east_rate, west_rate, north_rate, south_rate, vertical_mixing, vertical_mixing])


def apply_transpose(padded, rates_pad, retained):
    center = padded[..., 1:-1, 1:-1, 1:-1]
    summed = retained * center
    summed = summed + rates_pad[0, 1:-1, :-2, 1:-1] * padded[..., 1:-1, :-2, 1:-1]
    summed = summed + rates_pad[1, 1:-1, 2:, 1:-1] * padded[..., 1:-1, 2:, 1:-1]
    summed = summed + rates_pad[2, 1:-1, 1:-1, :-2] * padded[..., 1:-1, 1:-1, :-2]
    summed = summed + rates_pad[3, 1:-1, 1:-1, 2:] * padded[..., 1:-1, 1:-1, 2:]
    summed = summed + rates_pad[4, :-2, 1:-1, 1:-1] * padded[..., :-2, 1:-1, 1:-1]
    summed = summed + rates_pad[5, 2:, 1:-1, 1:-1] * padded[..., 2:, 1:-1, 1:-1]
    return summed


def reference(adjoint_iterate, innovations, station_cells, diffusivity, wind_x, wind_y, vertical_mixing):
    rate_fields = transfer_rates(diffusivity, wind_x, wind_y, vertical_mixing)
    retained = 1.0 - jnp.sum(rate_fields, axis=0)
    rates_pad = jnp.pad(rate_fields, ((0, 0), (1, 1), (1, 1), (1, 1)))
    tile_base = (jnp.arange(STATIONS_ALL, dtype=jnp.int32) // STATIONS) * (TX * NY)
    global_cells = (station_cells + tile_base[None, :]).astype(jnp.int32)

    def scatter_step(cell_ids, values):
        return jnp.zeros((LEV, NX * NY), jnp.float32).at[:, cell_ids].add(values)

    forcing = jax.vmap(scatter_step)(global_cells, innovations).reshape(STEPS, LEV, NX, NY)
    following = jnp.concatenate([adjoint_iterate[1:], jnp.zeros_like(adjoint_iterate[:1])], axis=0)
    following_pad = jnp.pad(following, ((0, 0), (1, 1), (1, 1), (1, 1)))
    residual = forcing - adjoint_iterate + apply_transpose(following_pad, rates_pad, retained)
    log_beta = math.log(circ_alpha) / STEPS
    step_index = jnp.arange(STEPS, dtype=jnp.float32)
    scaled = residual * jnp.exp(-step_index * log_beta)[:, None, None, None]
    spectrum = jnp.fft.fft(scaled, axis=0)
    source = jnp.stack([jnp.real(spectrum), jnp.imag(spectrum)])
    angles = step_index * (2.0 * math.pi / STEPS)
    cos_freq = jnp.cos(angles)[:, None, None, None]
    sin_freq = jnp.sin(angles)[:, None, None, None]
    beta_step = math.exp(log_beta)
    iterate = source
    for sweep_index in range(INNER):
        padded = jnp.pad(iterate, ((0, 0), (0, 0), (1, 1), (1, 1), (1, 1)))
        applied = apply_transpose(padded, rates_pad, retained)
        real_part = source[0] + beta_step * (cos_freq * applied[0] - sin_freq * applied[1])
        imag_part = source[1] + beta_step * (sin_freq * applied[0] + cos_freq * applied[1])
        iterate = jnp.stack([real_part, imag_part])
    restored = jnp.real(jnp.fft.ifft(iterate[0] + 1j * iterate[1], axis=0))
    correction = restored * jnp.exp(step_index * log_beta)[:, None, None, None]
    return adjoint_iterate + correction
```

```python
import functools

import jax
import jax.numpy as jnp
from jax import lax
from jax.experimental import pallas as pl
from jax.experimental.pallas import tpu as pltpu
from jax.sharding import PartitionSpec as P

MESH = pl.DeviceIdType.MESH

LEV = 16
TX = 8
NY = 128
STEPS_DEV = 8
DEPTH = 5
CIRC_ALPHA = 0.1

RATES, INNOV, CELLS, STATE, INNOV_UP, CELLS_UP, PER_SIDE = 0, 4, 5, 6, 14, 15, 16
INNOV_T, CELLS_T, STATE_T = 2 * PER_SIDE, 2 * PER_SIDE + 1, 2 * PER_SIDE + 2
TRANSFERS = STATE_T + DEPTH


def fill_forcing(forcing, which, plane, parts):
    x_of = lax.broadcasted_iota(jnp.int32, (TX, NY), 0)
    y_of = lax.broadcasted_iota(jnp.int32, (NY, NY), 0)
    total = None
    for values, cells, low, high in parts:
        column = cells // NY
        row = cells % NY
        mask = (column == x_of) & (x_of >= low) & (x_of < high)
        head = values.astype(jnp.bfloat16).astype(jnp.float32)
        rest = values - head
        pieces = [
            jnp.where(mask[None], piece[:, None, :], 0.0).reshape(LEV * TX, NY).astype(jnp.bfloat16)
            for piece in (head, rest)
        ]
        hot = jnp.where(row == y_of, 1.0, 0.0).astype(jnp.bfloat16)
        part = lax.dot_general(
            jnp.concatenate(pieces, axis=1),
            jnp.concatenate([hot, hot], axis=1),
            (((1,), (1,)), ((), ())),
            preferred_element_type=jnp.float32,
        )
        total = part if total is None else total + part
    forcing[plane, :, which] = total.reshape(LEV, TX, NY)


def kernel(
    time_parts, tiles,
    a, innov, cells, dif, wx, wy, vm, out,
    ac, hl, hr, a8, nc, nl, nr, kc, kl, kr, kc2, kl2, kr2, rc, rl, rr, coef, forcing, va, vb, ob,
    send, recv, local,
):
    t = lax.axis_index("tm")
    s = lax.axis_index("space")
    before = lax.rem(t + time_parts - 1, time_parts)
    after = lax.rem(t + 1, time_parts)
    has_left = s > 0
    has_right = s < tiles - 1
    is_last = t == time_parts - 1

    barrier = pltpu.get_barrier_semaphore()
    pl.semaphore_signal(barrier, inc=1, device_id=(after, s), device_id_type=MESH)

    @pl.when(has_left)
    def _():
        pl.semaphore_signal(barrier, inc=1, device_id=(t, s - 1), device_id_type=MESH)
        pl.semaphore_signal(barrier, inc=1, device_id=(after, s - 1), device_id_type=MESH)

    @pl.when(has_right)
    def _():
        pl.semaphore_signal(barrier, inc=1, device_id=(t, s + 1), device_id_type=MESH)
        pl.semaphore_signal(barrier, inc=1, device_id=(after, s + 1), device_id_type=MESH)

    fields = (dif, wx, wy, vm)
    loads = [
        pltpu.make_async_copy(innov, nc.at[pl.ds(0, STEPS_DEV)], local.at[0]),
        pltpu.make_async_copy(cells, kc, local.at[1]),
        pltpu.make_async_copy(a.at[pl.ds(DEPTH, 3)], ac.at[pl.ds(0, 3)], local.at[2]),
    ] + [pltpu.make_async_copy(f, rc.at[i], local.at[3 + i]) for i, f in enumerate(fields)]
    for load in loads:
        load.start()

    def remote(number, src, dst, device):
        return pltpu.make_async_remote_copy(
            src_ref=src, dst_ref=dst, send_sem=send.at[number], recv_sem=recv.at[number],
            device_id=device, device_id_type=MESH,
        )

    def side(base, step, first, width, halo, inn, cel, cel_up, rat):
        here, up = (t, s + step), (before, s + step)
        cols = pl.ds(first, width)
        edge = pl.ds(4, 4) if step > 0 else pl.ds(0, 4)
        rates = [
            remote(base + RATES + i, f.at[:, cols if i < 2 else edge], rat.at[i, :, cols if i < 2 else edge], here)
            for i, f in enumerate(fields)
        ]
        early = [
            remote(base + CELLS, cells, cel, here),
            remote(base + INNOV, innov, inn.at[pl.ds(0, STEPS_DEV)], here),
            remote(base + CELLS_UP, cells, cel_up, up),
            remote(base + INNOV_UP, innov.at[pl.ds(0, 4)], inn.at[pl.ds(STEPS_DEV, 4)], up),
        ]
        state = [
            remote(base + STATE + i, a.at[(i + DEPTH) % 8, :, cols], halo.at[i, :, cols], here if i < 3 else up)
            for i in range(8)
        ]
        return rates, early, state

    sides = (
        (has_right, has_left, side(0, 1, 3, 5, hl, nl, kl, kl2, rl)),
        (has_left, has_right, side(PER_SIDE, -1, 0, 5, hr, nr, kr, kr2, rr)),
    )
    up_early = [
        remote(CELLS_T, cells, kc2, (before, s)),
        remote(INNOV_T, innov.at[pl.ds(0, 4)], nc.at[pl.ds(STEPS_DEV, 4)], (before, s)),
    ]
    up_state = [remote(STATE_T + i, a.at[i], ac.at[3 + i], (before, s)) for i in range(DEPTH)]

    for has, (halo, inn, cel, cel_up, rat) in (
        (has_left, (hl, nl, kl, kl2, rl)),
        (has_right, (hr, nr, kr, kr2, rr)),
    ):

        @pl.when(jnp.logical_not(has))
        def _(refs=(halo, inn, cel, cel_up, rat)):
            for ref in refs:
                ref[...] = jnp.zeros_like(ref)

    neighbours = 1 + 2 * has_left.astype(jnp.int32) + 2 * has_right.astype(jnp.int32)
    pl.semaphore_wait(barrier, neighbours)
    for part in range(3):
        for sends, _, groups in sides:

            @pl.when(sends)
            def _(copies=groups[part]):
                for copy in copies:
                    copy.start()

        for copy in ([], up_early, up_state)[part]:
            copy.start()

    for load in loads:
        load.wait()

    def own_forcing(n, carry):
        fill_forcing(forcing, 0, n, [(nc[n], kc[pl.ds(n, 1)], 0, TX)])
        return carry

    lax.fori_loop(0, STEPS_DEV, own_forcing, 0)

    for _, receives, (rates, early, _) in sides:

        @pl.when(receives)
        def _(copies=rates + early):
            for copy in copies:
                copy.wait_recv()

    for copy in up_early:
        copy.wait_recv()

    x_of = lax.broadcasted_iota(jnp.int32, (TX, NY), 0)
    y_of = lax.broadcasted_iota(jnp.int32, (TX, NY), 1)
    first_half = x_of < 4
    is_first, is_end = x_of == 0, x_of == TX - 1

    def down_x(v):
        return pltpu.roll(v, 1, 0)

    def up_x(v):
        return pltpu.roll(v, TX - 1, 0)

    def make_rates(l, carry):
        def own(part):
            return part[0, l], part[1, l], part[2, l], part[3, l]

        dc, xc, yc, mc = own(rc)
        dl, xl, yl, ml = own(rl)
        dr, xr, yr, mr = own(rr)
        east_c, west_c = dc + jnp.maximum(-xc, 0.0), dc + jnp.maximum(xc, 0.0)
        east_l, west_l = dl + jnp.maximum(-xl, 0.0), dl + jnp.maximum(xl, 0.0)
        east_r, west_r = dr + jnp.maximum(-xr, 0.0), dr + jnp.maximum(xr, 0.0)
        dh = jnp.where(first_half, dr, dl)
        yh = jnp.where(first_half, yr, yl)
        mh = jnp.where(first_half, mr, ml)
        east_h = jnp.where(first_half, east_r, east_l)
        west_h = jnp.where(first_half, west_r, west_l)
        from_west = (
            jnp.where(is_first, down_x(east_l), down_x(east_c)),
            jnp.where(first_half, jnp.where(is_first, down_x(east_c), down_x(east_r)), down_x(east_l)),
        )
        from_east = (
            jnp.where(is_end, up_x(west_r), up_x(west_c)),
            jnp.where(first_half, up_x(west_r), jnp.where(is_end, up_x(west_c), up_x(west_l))),
        )
        for which, (d, e, w, y, m) in enumerate(
            ((dc, east_c, west_c, yc, mc), (dh, east_h, west_h, yh, mh))
        ):
            north, south = d + jnp.maximum(-y, 0.0), d + jnp.maximum(y, 0.0)
            coef[l, which, 0] = 1.0 - (e + w + north + south + m + m)
            coef[l, which, 1] = from_west[which]
            coef[l, which, 2] = from_east[which]
            coef[l, which, 3] = jnp.where(y_of == 0, 0.0, pltpu.roll(north, 1, 1))
            coef[l, which, 4] = jnp.where(y_of == NY - 1, 0.0, pltpu.roll(south, NY - 1, 1))
            coef[l, which, 5] = m
        return carry

    lax.fori_loop(0, LEV, make_rates, 0)

    def halo_forcing(n, carry):
        fill_forcing(forcing, 1, n, [(nl[n], kl[pl.ds(n, 1)], 4, TX), (nr[n], kr[pl.ds(n, 1)], 0, 4)])
        return carry

    lax.fori_loop(1, STEPS_DEV, halo_forcing, 0)

    def next_forcing(n, carry):
        m = n + STEPS_DEV
        fill_forcing(forcing, 0, m, [(nc[m], kc2[pl.ds(n, 1)], 0, TX)])
        fill_forcing(forcing, 1, m, [(nl[m], kl2[pl.ds(n, 1)], 4, TX), (nr[m], kr2[pl.ds(n, 1)], 0, 4)])
        return carry

    lax.fori_loop(0, 4, next_forcing, 0)

    def spread(l, which, v, west, east, force):
        total = force + coef[l, which, 0] * v
        total = total + coef[l, which, 1] * west
        total = total + coef[l, which, 2] * east
        total = total + coef[l, which, 3] * pltpu.roll(v, 1, 1)
        return total + coef[l, which, 4] * pltpu.roll(v, NY - 1, 1)

    def sweep(i, src, dst, plane, last):
        for l in range(LEV):
            c, h = src(l)
            cd, cu = down_x(c), up_x(c)
            if isinstance(h, tuple):
                left, right = h
                ld, rd, lu, ru = down_x(left), down_x(right), up_x(left), up_x(right)
                h = jnp.where(first_half, right, left)
                hd = jnp.where(first_half, rd, ld)
                hu = jnp.where(first_half, ru, lu)
                west_c, east_c = jnp.where(is_first, ld, cd), jnp.where(is_end, ru, cu)
            else:
                hd, hu = down_x(h), up_x(h)
                west_c, east_c = jnp.where(is_first, hd, cd), jnp.where(is_end, hu, cu)
            west_h, east_h = jnp.where(is_first, cd, hd), jnp.where(is_end, cu, hu)
            for which, (v, west, east) in enumerate(((c, west_c, east_c), (h, west_h, east_h))):
                if last and which:
                    continue
                total = spread(l, which, v, west, east, forcing[plane, l, which])
                for k in (l - 1, l + 1):
                    if 0 <= k < LEV:
                        o = src(k)[which]
                        if isinstance(o, tuple):
                            o = jnp.where(first_half, o[1], o[0])
                        total = total + coef[k, which, 5] * o
                if last:
                    ob[i, l] = total
                else:
                    dst[l, which] = total

    def chain(i, carry):
        for _, receives, (_, _, state) in sides:

            @pl.when(receives)
            def _(state=state):
                for k in range(8):

                    @pl.when(i == k)
                    def _(copy=state[k]):
                        copy.wait_recv()

        for k in range(DEPTH):

            @pl.when(i == k + 3)
            def _(copy=up_state[k]):
                copy.wait_recv()

        @pl.when(is_last & (i == 3))
        def _():
            a8[:, 0] = ac[3]
            for l in range(LEV):
                a8[l, 1] = jnp.where(first_half, hr[3, l], hl[3, l])
            for ref in (ac, hl, hr):
                ref[3] = jnp.zeros((LEV, TX, NY), jnp.float32)

        sweep(i, lambda l: (ac[i, l], (hl[i, l], hr[i, l])), va, i + 4, False)
        bufs = (va, vb)
        for k in range(2, DEPTH + 1):
            src, dst = bufs[k % 2], bufs[(k + 1) % 2]

            @pl.when(is_last & (i == k + 2))
            def _(src=src):
                src[...] = CIRC_ALPHA * (src[...] - a8[...])

            sweep(i, lambda l, src=src: (src[l, 0], src[l, 1]), dst, i + DEPTH - k, k == DEPTH)
        pltpu.make_async_copy(ob.at[i], out.at[i], local.at[7 + i]).start()
        return carry

    lax.fori_loop(0, STEPS_DEV, chain, 0)

    for i in range(STEPS_DEV):
        pltpu.make_async_copy(ob.at[i], out.at[i], local.at[7 + i]).wait()
    for sends, _, groups in sides:

        @pl.when(sends)
        def _(copies=groups[0] + groups[1] + groups[2]):
            for copy in copies:
                copy.wait_send()

    for copy in up_early + up_state:
        copy.wait_send()


def body(adjoint_iterate, innovations, station_cells, diffusivity, wind_x, wind_y, vertical_mixing):
    field = (LEV, TX, NY)
    f32, i32 = jnp.float32, jnp.int32
    scratch = (
        [pltpu.VMEM((STEPS_DEV,) + field, f32)] * 3
        + [pltpu.VMEM((LEV, 2, TX, NY), f32)]
        + [pltpu.VMEM((STEPS_DEV + 4, LEV, NY), f32)] * 3
        + [pltpu.VMEM((STEPS_DEV, NY), i32)] * 6
        + [pltpu.VMEM((4,) + field, f32)] * 3
        + [pltpu.VMEM((LEV, 2, 6, TX, NY), f32)]
        + [pltpu.VMEM((STEPS_DEV + 4, LEV, 2, TX, NY), f32)]
        + [pltpu.VMEM((LEV, 2, TX, NY), f32)] * 2
        + [pltpu.VMEM((STEPS_DEV,) + field, f32)]
        + [pltpu.SemaphoreType.DMA((TRANSFERS,))] * 2
        + [pltpu.SemaphoreType.DMA((7 + STEPS_DEV,))]
    )
    return pl.pallas_call(
        functools.partial(kernel, lax.axis_size("tm"), lax.axis_size("space")),
        out_shape=jax.ShapeDtypeStruct((STEPS_DEV,) + field, f32),
        in_specs=[pl.BlockSpec(memory_space=pl.ANY)] * 7,
        out_specs=pl.BlockSpec(memory_space=pl.ANY),
        scratch_shapes=scratch,
        compiler_params=pltpu.CompilerParams(
            collective_id=0, has_side_effects=True, vmem_limit_bytes=24 * 2**20
        ),
        name="update",
    )(adjoint_iterate, innovations, station_cells, diffusivity, wind_x, wind_y, vertical_mixing)


def solution(mesh):
    in_specs = (
        P("tm", None, "space", None),
        P("tm", None, "space"),
        P("tm", "space"),
        P(None, "space", None),
        P(None, "space", None),
        P(None, "space", None),
        P(None, "space", None),
    )
    out_specs = P("tm", None, "space", None)
    return jax.shard_map(body, mesh=mesh, in_specs=in_specs, out_specs=out_specs, check_vma=False)
```

```python
import functools

import jax
import jax.numpy as jnp
from jax import lax
from jax.experimental import pallas as pl
from jax.experimental.pallas import tpu as pltpu
from jax.sharding import PartitionSpec as P

MESH = pl.DeviceIdType.MESH

LEV = 16
TX = 8
NY = 128
STEPS_DEV = 8
DEPTH = 5
CIRC_ALPHA = 0.1

RATES, FORWARD, INNOV, CELLS, STATE, INNOV_UP, CELLS_UP, RELAY, PER_SIDE = 0, 4, 8, 9, 10, 18, 19, 20, 25
INNOV_T, CELLS_T, STATE_T = 2 * PER_SIDE, 2 * PER_SIDE + 1, 2 * PER_SIDE + 2
TRANSFERS = STATE_T + DEPTH
OWN = STEPS_DEV - DEPTH


def fill_forcing(forcing, which, plane, parts):
    x_of = lax.broadcasted_iota(jnp.int32, (TX, NY), 0)
    y_of = lax.broadcasted_iota(jnp.int32, (NY, NY), 0)
    total = None
    for values, cells, low, high in parts:
        column = cells // NY
        row = cells % NY
        mask = (column == x_of) & (x_of >= low) & (x_of < high)
        head = values.astype(jnp.bfloat16).astype(jnp.float32)
        rest = values - head
        pieces = [
            jnp.where(mask[None], piece[:, None, :], 0.0).reshape(LEV * TX, NY).astype(jnp.bfloat16)
            for piece in (head, rest)
        ]
        hot = jnp.where(row == y_of, 1.0, 0.0).astype(jnp.bfloat16)
        part = lax.dot_general(
            jnp.concatenate(pieces, axis=1),
            jnp.concatenate([hot, hot], axis=1),
            (((1,), (1,)), ((), ())),
            preferred_element_type=jnp.float32,
        )
        total = part if total is None else total + part
    forcing[plane, :, which] = total.reshape(LEV, TX, NY)


def kernel(
    time_parts, tiles,
    a, innov, cells, dif, wx, wy, vm, out,
    ac, hl, hr, nc, nl, nr, kc, kl, kr, kc2, kl2, kr2, rc, rl, rr, coef, forcing, va, vb, ob,
    send, recv, local,
):
    t = lax.axis_index("tm")
    s = lax.axis_index("space")
    before = lax.rem(t + time_parts - 1, time_parts)
    after = lax.rem(t + 1, time_parts)
    core = lax.rem(t, 2)
    sibling = t + 1 - 2 * core
    mid = tiles // 2
    has_left = s > 0
    has_right = s < tiles - 1
    is_last = t == time_parts - 1

    barrier = pltpu.get_barrier_semaphore()

    def greet(device):
        pl.semaphore_signal(barrier, inc=1, device_id=device, device_id_type=MESH)

    greet((after, s))
    greet((sibling, s))
    for here, device in (
        (has_left, s - 1),
        (has_right, s + 1),
        (s == 0, mid - 1),
        (s == tiles - 1, mid),
        (s == mid, 0),
        (s == mid - 1, tiles - 1),
    ):

        @pl.when(here)
        def _(device=device):
            greet((t, device))

    fields = (dif, wx, wy, vm)
    loads = [
        pltpu.make_async_copy(innov, nc.at[pl.ds(0, STEPS_DEV)], local.at[0]),
        pltpu.make_async_copy(cells, kc, local.at[1]),
        pltpu.make_async_copy(a.at[pl.ds(DEPTH, OWN)], ac.at[pl.ds(0, OWN)], local.at[2]),
    ] + [pltpu.make_async_copy(f, rc.at[i], local.at[3 + i]) for i, f in enumerate(fields)]
    for load in loads:
        load.start()

    def remote(number, src, dst, device, landing=None):
        return pltpu.make_async_remote_copy(
            src_ref=src, dst_ref=dst, send_sem=send.at[number],
            recv_sem=recv.at[number if landing is None else landing],
            device_id=device, device_id_type=MESH,
        )

    class Side:
        def __init__(self, base, step, first, halo, inn, cel, cel_up, rat, relay, entry):
            self.sends, self.receives = (has_right, has_left) if step > 0 else (has_left, has_right)
            self.zeros = (halo.at[pl.ds(0, OWN)], inn, cel, cel_up, rat)
            to = (t, s + step)
            cols = pl.ds(first, 5)
            edge = pl.ds(4, 4) if step > 0 else pl.ds(0, 4)
            cut = [cols if i < 2 else edge for i in range(4)]
            self.rates = [
                remote(base + RATES + i, f.at[:, cut[i]], rat.at[i, :, cut[i]], to)
                for i, f in enumerate(fields)
            ]
            self.forward = [
                remote(base + FORWARD + i, rat.at[i, :, cut[i]], rat.at[i, :, cut[i]], (sibling, s), base + RATES + i)
                for i in range(4)
            ]
            self.early = [
                remote(base + CELLS, cells, cel, to),
                remote(base + INNOV, innov, inn.at[pl.ds(0, STEPS_DEV)], to),
            ]
            self.late = [
                remote(base + CELLS_UP, kc2, cel_up, to),
                remote(base + INNOV_UP, nc.at[pl.ds(STEPS_DEV, 4)], inn.at[pl.ds(STEPS_DEV, 4)], to),
            ]
            self.is_relay = s == relay
            late_to = (t, jnp.where(s == entry, relay, s + step))
            self.state = [
                remote(base + STATE + i, a.at[i + DEPTH, :, cols], halo.at[i, :, cols], to)
                for i in range(OWN)
            ] + [
                remote(base + STATE + i, ac.at[i, :, cols], halo.at[i, :, cols], late_to)
                for i in range(OWN, STEPS_DEV)
            ]
            self.relayed = [
                remote(base + RELAY + i - OWN, halo.at[i, :, cols], halo.at[i, :, cols], (t, entry + step), base + STATE + i)
                for i in range(OWN, STEPS_DEV)
            ]

    sides = (
        Side(0, 1, 3, hl, nl, kl, kl2, rl, 0, mid - 1),
        Side(PER_SIDE, -1, 0, hr, nr, kr, kr2, rr, tiles - 1, mid),
    )
    up_early = [
        remote(CELLS_T, cells, kc2, (before, s)),
        remote(INNOV_T, innov.at[pl.ds(0, 4)], nc.at[pl.ds(STEPS_DEV, 4)], (before, s)),
    ]
    up_state = [remote(STATE_T + i, a.at[i], ac.at[OWN + i], (before, s)) for i in range(DEPTH)]

    for side in sides:

        @pl.when(jnp.logical_not(side.receives))
        def _(side=side):
            for ref in side.zeros:
                ref[...] = jnp.zeros(ref.shape, ref.dtype)

    def each(condition, copies, act):
        @pl.when(condition)
        def _():
            for copy in copies:
                act(copy)

    def begin(copy):
        copy.start()

    def arrive(copy):
        copy.wait_recv()

    def leave(copy):
        copy.wait_send()

    def number(flag):
        return flag.astype(jnp.int32)

    pl.semaphore_wait(
        barrier,
        2 + number(has_left) + number(has_right) + number(s == 0) + number(s == tiles - 1)
        + number(s == mid) + number(s == mid - 1),
    )
    for copy in up_early + up_state:
        copy.start()
    for side in sides:
        each(side.sends, side.early, begin)
    for side in sides:
        for half in range(2):
            each(side.sends & (core == half), side.rates[2 * half : 2 * half + 2], begin)
    for i in range(OWN):
        for side in sides:
            each(side.sends, [side.state[i]], begin)

    for load in loads:
        load.wait()

    def own_forcing(n, carry):
        fill_forcing(forcing, 0, n, [(nc[n], kc[pl.ds(n, 1)], 0, TX)])
        return carry

    lax.fori_loop(0, STEPS_DEV, own_forcing, 0)

    def pass_on():
        for copy in up_early:
            copy.wait_recv()
        for side in sides:
            each(side.sends, side.late, begin)
        for i in range(DEPTH):
            up_state[i].wait_recv()
            for side in sides:
                each(side.sends, [side.state[OWN + i]], begin)

    pl.when(core == 0)(pass_on)

    for side in sides:
        for half in range(2):
            mine = slice(2 * half, 2 * half + 2)
            each(side.receives & (core == half), side.rates[mine], arrive)
            each(side.receives & (core == half), side.forward[mine], begin)
    for side in sides:
        for half in range(2):
            other = slice(2 - 2 * half, 4 - 2 * half)
            each(side.receives & (core == half), side.rates[other], arrive)

    x_of = lax.broadcasted_iota(jnp.int32, (TX, NY), 0)
    y_of = lax.broadcasted_iota(jnp.int32, (TX, NY), 1)
    first_half = x_of < 4
    is_first, is_end = x_of == 0, x_of == TX - 1

    def down_x(v):
        return pltpu.roll(v, 1, 0)

    def up_x(v):
        return pltpu.roll(v, TX - 1, 0)

    def make_rates(l, carry):
        def own(part):
            return part[0, l], part[1, l], part[2, l], part[3, l]

        dc, xc, yc, mc = own(rc)
        dl, xl, yl, ml = own(rl)
        dr, xr, yr, mr = own(rr)
        east_c, west_c = dc + jnp.maximum(-xc, 0.0), dc + jnp.maximum(xc, 0.0)
        east_l, west_l = dl + jnp.maximum(-xl, 0.0), dl + jnp.maximum(xl, 0.0)
        east_r, west_r = dr + jnp.maximum(-xr, 0.0), dr + jnp.maximum(xr, 0.0)
        dh = jnp.where(first_half, dr, dl)
        yh = jnp.where(first_half, yr, yl)
        mh = jnp.where(first_half, mr, ml)
        east_h = jnp.where(first_half, east_r, east_l)
        west_h = jnp.where(first_half, west_r, west_l)
        from_west = (
            jnp.where(is_first, down_x(east_l), down_x(east_c)),
            jnp.where(first_half, jnp.where(is_first, down_x(east_c), down_x(east_r)), down_x(east_l)),
        )
        from_east = (
            jnp.where(is_end, up_x(west_r), up_x(west_c)),
            jnp.where(first_half, up_x(west_r), jnp.where(is_end, up_x(west_c), up_x(west_l))),
        )
        for which, (d, e, w, y, m) in enumerate(
            ((dc, east_c, west_c, yc, mc), (dh, east_h, west_h, yh, mh))
        ):
            north, south = d + jnp.maximum(-y, 0.0), d + jnp.maximum(y, 0.0)
            coef[l, which, 0] = 1.0 - (e + w + north + south + m + m)
            coef[l, which, 1] = from_west[which]
            coef[l, which, 2] = from_east[which]
            coef[l, which, 3] = jnp.where(y_of == 0, 0.0, pltpu.roll(north, 1, 1))
            coef[l, which, 4] = jnp.where(y_of == NY - 1, 0.0, pltpu.roll(south, NY - 1, 1))
            coef[l, which, 5] = m
        return carry

    lax.fori_loop(0, LEV, make_rates, 0)

    for side in sides:
        each(side.receives, side.early, arrive)

    def halo_forcing(n, carry):
        fill_forcing(forcing, 1, n, [(nl[n], kl[pl.ds(n, 1)], 4, TX), (nr[n], kr[pl.ds(n, 1)], 0, 4)])
        return carry

    lax.fori_loop(1, STEPS_DEV, halo_forcing, 0)
    pl.when(core == 1)(pass_on)

    def next_forcing(n):
        m = n + STEPS_DEV
        fill_forcing(forcing, 0, m, [(nc[m], kc2[pl.ds(n, 1)], 0, TX)])
        fill_forcing(forcing, 1, m, [(nl[m], kl2[pl.ds(n, 1)], 4, TX), (nr[m], kr2[pl.ds(n, 1)], 0, 4)])

    def sweep(i, load, dst, plane, last):
        def level(l):
            c, h = load(l)
            whole = h
            if isinstance(h, tuple):
                whole = jnp.where(first_half, h[1], h[0])
            tiles = [(c, whole), (coef[l, 0, 5] * c, None if last else coef[l, 1, 5] * whole)]
            return c, h, whole, tiles[1]

        levels = [level(0), level(1)]
        for l in range(LEV):
            if 0 < l < LEV - 1:
                levels.append(level(l + 1))
            c, h, whole, _ = levels[l]
            cd, cu = down_x(c), up_x(c)
            if isinstance(h, tuple):
                ld, rd, lu, ru = down_x(h[0]), down_x(h[1]), up_x(h[0]), up_x(h[1])
                hd, hu = jnp.where(first_half, rd, ld), jnp.where(first_half, ru, lu)
            else:
                hd, hu = down_x(whole), up_x(whole)
                ld, ru = hd, hu
            todo = [(0, c, jnp.where(is_first, ld, cd), jnp.where(is_end, ru, cu))]
            if not last:
                todo.append((1, whole, jnp.where(is_first, cd, hd), jnp.where(is_end, cu, hu)))
            for which, v, west, east in todo:
                total = forcing[plane, l, which] + coef[l, which, 0] * v
                total = total + (coef[l, which, 1] * west + coef[l, which, 2] * east)
                total = total + (
                    coef[l, which, 3] * pltpu.roll(v, 1, 1) + coef[l, which, 4] * pltpu.roll(v, NY - 1, 1)
                )
                for k in (l - 1, l + 1):
                    if 0 <= k < LEV:
                        total = total + levels[k][3][which]
                if last:
                    ob[i, l] = total
                else:
                    dst[l, which] = total

    def chain(i, carry):
        for k in range(STEPS_DEV):
            for side in sides:
                each(side.receives & (i == k), [side.state[k]], arrive)

        @pl.when(i == OWN)
        def _():
            for k in range(DEPTH):
                for side in sides:
                    each(side.is_relay, [side.state[OWN + k]], arrive)
                    each(side.is_relay, [side.relayed[k]], begin)

        @pl.when(i == OWN + 1)
        def _():
            for side in sides:
                each(side.receives, side.late, arrive)

        @pl.when(i > OWN)
        def _():
            next_forcing(i - OWN - 1)

        sweep(i, lambda l: (ac[i, l], (hl[i, l], hr[i, l])), va, i + 4, False)

        @pl.when(is_last & (i == OWN))
        def _():
            va[...] = forcing[STEPS_DEV - 1]

        bufs = (va, vb)
        for k in range(2, DEPTH + 1):
            src, dst = bufs[k % 2], bufs[(k + 1) % 2]

            @pl.when(is_last & (i == k + 2))
            def _(src=src):
                src[:, 0] = CIRC_ALPHA * (src[:, 0] - ac[OWN])
                outside = jnp.where(first_half[None], hr[OWN], hl[OWN])
                src[:, 1] = CIRC_ALPHA * (src[:, 1] - outside)

            sweep(i, lambda l, src=src: (src[l, 0], src[l, 1]), dst, i + DEPTH - k, k == DEPTH)
        pltpu.make_async_copy(ob.at[i], out.at[i], local.at[7 + i]).start()
        return carry

    lax.fori_loop(0, STEPS_DEV, chain, 0)

    for i in range(STEPS_DEV):
        pltpu.make_async_copy(ob.at[i], out.at[i], local.at[7 + i]).wait()
    for side in sides:
        each(side.sends, side.early + side.late + side.state, leave)
        each(side.is_relay, side.relayed, leave)
        for half in range(2):
            mine = slice(2 * half, 2 * half + 2)
            each(side.sends & (core == half), side.rates[mine], leave)
            each(side.receives & (core == half), side.forward[mine], leave)
    for copy in up_early + up_state:
        copy.wait_send()


def body(adjoint_iterate, innovations, station_cells, diffusivity, wind_x, wind_y, vertical_mixing):
    field = (LEV, TX, NY)
    f32, i32 = jnp.float32, jnp.int32
    scratch = (
        [pltpu.VMEM((STEPS_DEV,) + field, f32)] * 3
        + [pltpu.VMEM((STEPS_DEV + 4, LEV, NY), f32)] * 3
        + [pltpu.VMEM((STEPS_DEV, NY), i32)] * 6
        + [pltpu.VMEM((4,) + field, f32)] * 3
        + [pltpu.VMEM((LEV, 2, 6, TX, NY), f32)]
        + [pltpu.VMEM((STEPS_DEV + 4, LEV, 2, TX, NY), f32)]
        + [pltpu.VMEM((LEV, 2, TX, NY), f32)] * 2
        + [pltpu.VMEM((STEPS_DEV,) + field, f32)]
        + [pltpu.SemaphoreType.DMA((TRANSFERS,))] * 2
        + [pltpu.SemaphoreType.DMA((7 + STEPS_DEV,))]
    )
    return pl.pallas_call(
        functools.partial(kernel, lax.axis_size("tm"), lax.axis_size("space")),
        out_shape=jax.ShapeDtypeStruct((STEPS_DEV,) + field, f32),
        in_specs=[pl.BlockSpec(memory_space=pl.ANY)] * 7,
        out_specs=pl.BlockSpec(memory_space=pl.ANY),
        scratch_shapes=scratch,
        compiler_params=pltpu.CompilerParams(
            collective_id=0, has_side_effects=True, vmem_limit_bytes=62 * 2**20
        ),
        name="update",
    )(adjoint_iterate, innovations, station_cells, diffusivity, wind_x, wind_y, vertical_mixing)


def solution(mesh):
    in_specs = (
        P("tm", None, "space", None),
        P("tm", None, "space"),
        P("tm", "space"),
        P(None, "space", None),
        P(None, "space", None),
        P(None, "space", None),
        P(None, "space", None),
    )
    out_specs = P("tm", None, "space", None)
    return jax.shard_map(body, mesh=mesh, in_specs=in_specs, out_specs=out_specs, check_vma=False)
```

```python
import functools

import jax
import jax.numpy as jnp
from jax import lax
from jax.experimental import pallas as pl
from jax.experimental.pallas import tpu as pltpu
from jax.sharding import PartitionSpec as P

MESH = pl.DeviceIdType.MESH

LEV = 16
TX = 8
NY = 128
STEPS_DEV = 8
DEPTH = 5
CIRC_ALPHA = 0.1
GROUP = 2

RATES, FORWARD, INNOV, CELLS, STATE, INNOV_UP, CELLS_UP, RELAY, PER_SIDE = 0, 4, 8, 9, 10, 18, 19, 20, 23
INNOV_T, CELLS_T, STATE_T = 2 * PER_SIDE, 2 * PER_SIDE + 1, 2 * PER_SIDE + 2
TRANSFERS = STATE_T + DEPTH
OWN = STEPS_DEV - DEPTH


def fill_forcing(forcing, which, plane, parts):
    x_of = lax.broadcasted_iota(jnp.int32, (TX, NY), 0)
    y_of = lax.broadcasted_iota(jnp.int32, (NY, NY), 0)
    total = None
    for values, cells, low, high in parts:
        column = cells // NY
        row = cells % NY
        mask = (column == x_of) & (x_of >= low) & (x_of < high)
        head = values.astype(jnp.bfloat16).astype(jnp.float32)
        rest = values - head
        pieces = [
            jnp.where(mask[None], piece[:, None, :], 0.0).reshape(LEV * TX, NY).astype(jnp.bfloat16)
            for piece in (head, rest)
        ]
        hot = jnp.where(row == y_of, 1.0, 0.0).astype(jnp.bfloat16)
        part = lax.dot_general(
            jnp.concatenate(pieces, axis=1),
            jnp.concatenate([hot, hot], axis=1),
            (((1,), (1,)), ((), ())),
            preferred_element_type=jnp.float32,
        )
        total = part if total is None else total + part
    forcing[plane, :, which] = total.reshape(LEV, TX, NY)


def kernel(
    time_parts, tiles,
    a, innov, cells, dif, wx, wy, vm, out,
    ac, hl, hr, nc, nl, nr, kc, kl, kr, kc2, kl2, kr2, rc, rl, rr, coef, forcing, va, vb, ob, hold,
    send, recv, local, ready,
):
    t = lax.axis_index("tm")
    s = lax.axis_index("space")
    before = lax.rem(t + time_parts - 1, time_parts)
    after = lax.rem(t + 1, time_parts)
    core = lax.rem(t, 2)
    sibling = t + 1 - 2 * core
    mid = tiles // 2
    has_left = s > 0
    has_right = s < tiles - 1
    is_last = t == time_parts - 1

    barrier = pltpu.get_barrier_semaphore()

    def greet(device):
        pl.semaphore_signal(barrier, inc=1, device_id=device, device_id_type=MESH)

    greet((after, s))
    greet((sibling, s))
    for here, device in (
        (has_left, s - 1),
        (has_right, s + 1),
        (s == 0, mid - 1),
        (s == 0, mid),
        (s == tiles - 1, mid - 1),
        (s == mid, tiles - 1),
    ):

        @pl.when(here)
        def _(device=device):
            greet((t, device))

    fields = (dif, wx, wy, vm)
    loads = [
        pltpu.make_async_copy(innov, nc.at[pl.ds(0, STEPS_DEV)], local.at[0]),
        pltpu.make_async_copy(cells, kc, local.at[1]),
        pltpu.make_async_copy(a.at[pl.ds(DEPTH, OWN)], ac.at[pl.ds(0, OWN)], local.at[2]),
    ] + [pltpu.make_async_copy(f, rc.at[i], local.at[3 + i]) for i, f in enumerate(fields)]
    for load in loads:
        load.start()

    def remote(number, src, dst, device, landing=None):
        return pltpu.make_async_remote_copy(
            src_ref=src, dst_ref=dst, send_sem=send.at[number],
            recv_sem=recv.at[number if landing is None else landing],
            device_id=device, device_id_type=MESH,
        )

    class Side:
        def __init__(self, base, step, first, halo, inn, cel, cel_up, rat, relay, entry):
            self.sends, self.receives = (has_right, has_left) if step > 0 else (has_left, has_right)
            self.zeros = (halo, inn, cel, cel_up, rat)
            to = (t, s + step)
            cols = pl.ds(first, 5)
            edge = pl.ds(4, 4) if step > 0 else pl.ds(0, 4)
            cut = [cols if i < 2 else edge for i in range(4)]
            self.rates = [
                remote(base + RATES + i, f.at[:, cut[i]], rat.at[i, :, cut[i]], to)
                for i, f in enumerate(fields)
            ]
            self.forward = [
                remote(base + FORWARD + i, rat.at[i, :, cut[i]], rat.at[i, :, cut[i]], (sibling, s), base + RATES + i)
                for i in range(4)
            ]
            self.early = [
                remote(base + CELLS, cells, cel, to),
                remote(base + INNOV, innov, inn.at[pl.ds(0, STEPS_DEV)], to),
            ]
            self.late = [
                remote(base + CELLS_UP, kc2, cel_up, to),
                remote(base + INNOV_UP, nc.at[pl.ds(STEPS_DEV, 4)], inn.at[pl.ds(STEPS_DEV, 4)], to),
            ]
            self.is_relay, self.is_entry = s == relay, s == entry
            self.state = [
                remote(base + STATE + i, a.at[i + DEPTH, :, cols], halo.at[i, :, cols], to)
                for i in range(OWN)
            ] + [
                remote(base + STATE + i, ac.at[i, :, cols], halo.at[i, :, cols], to)
                for i in range(OWN, STEPS_DEV)
            ]
            self.detour = [
                remote(base + STATE + i, a.at[i + DEPTH, :, cols], hold.at[i, :, cols], (t, relay), base + RELAY + i)
                for i in range(OWN)
            ]
            self.relayed = [
                remote(base + RELAY + i, hold.at[i, :, cols], halo.at[i, :, cols], (t, entry + step), base + STATE + i)
                for i in range(OWN)
            ]

    sides = (
        Side(0, 1, 3, hl, nl, kl, kl2, rl, tiles - 1, mid - 1),
        Side(PER_SIDE, -1, 0, hr, nr, kr, kr2, rr, 0, mid),
    )
    up_early = [
        remote(CELLS_T, cells, kc2, (before, s)),
        remote(INNOV_T, innov.at[pl.ds(0, 4)], nc.at[pl.ds(STEPS_DEV, 4)], (before, s)),
    ]
    up_state = [remote(STATE_T + i, a.at[i], ac.at[OWN + i], (before, s)) for i in range(DEPTH)]

    for side in sides:

        @pl.when(jnp.logical_not(side.receives))
        def _(side=side):
            for ref in side.zeros:
                ref[...] = jnp.zeros(ref.shape, ref.dtype)

    def each(condition, copies, act):
        @pl.when(condition)
        def _():
            for copy in copies:
                act(copy)

    def begin(copy):
        copy.start()

    def arrive(copy):
        copy.wait_recv()

    def leave(copy):
        copy.wait_send()

    def number(flag):
        return flag.astype(jnp.int32)

    pl.semaphore_wait(
        barrier,
        2 + number(has_left) + number(has_right) + 2 * number(s == mid - 1) + number(s == mid)
        + number(s == tiles - 1),
    )

    @pl.when(s == mid - 1)
    def _():
        pl.semaphore_signal(ready, inc=1, device_id=(t, 0), device_id_type=MESH)

    for copy in up_early + up_state:
        copy.start()
    for side in sides:
        each(side.sends, side.early, begin)
        each(side.is_entry, side.detour, begin)
    for side in sides:
        for half in range(2):
            each(side.sends & (core == half), side.rates[2 * half : 2 * half + 2], begin)

    for load in loads:
        load.wait()
    for i in range(OWN):
        for side in sides:
            each(side.sends & jnp.logical_not(side.is_entry), [side.state[i]], begin)

    def own_forcing(n, carry):
        fill_forcing(forcing, 0, n, [(nc[n], kc[pl.ds(n, 1)], 0, TX)])
        return carry

    lax.fori_loop(0, STEPS_DEV, own_forcing, 0, unroll=4)

    def pass_on(first, last):
        if first == 0:
            for copy in up_early:
                copy.wait_recv()
            for side in sides:
                each(side.sends, side.late, begin)
        for i in range(first, last):
            up_state[i].wait_recv()
            for side in sides:
                each(side.sends, [side.state[OWN + i]], begin)

    @pl.when(core == 0)
    def _():
        pass_on(0, DEPTH)

    for side in sides:
        for half in range(2):
            mine = slice(2 * half, 2 * half + 2)
            each(side.receives & (core == half), side.rates[mine], arrive)
            each(side.receives & (core == half), side.forward[mine], begin)
    for side in sides:
        for half in range(2):
            other = slice(2 - 2 * half, 4 - 2 * half)
            each(side.receives & (core == half), side.rates[other], arrive)

    x_of = lax.broadcasted_iota(jnp.int32, (TX, NY), 0)
    y_of = lax.broadcasted_iota(jnp.int32, (TX, NY), 1)
    first_half = x_of < 4
    is_first, is_end = x_of == 0, x_of == TX - 1

    def down_x(v):
        return pltpu.roll(v, 1, 0)

    def up_x(v):
        return pltpu.roll(v, TX - 1, 0)

    def make_rates(l, carry):
        def own(part):
            return part[0, l], part[1, l], part[2, l], part[3, l]

        dc, xc, yc, mc = own(rc)
        dl, xl, yl, ml = own(rl)
        dr, xr, yr, mr = own(rr)
        east_c, west_c = dc + jnp.maximum(-xc, 0.0), dc + jnp.maximum(xc, 0.0)
        east_l, west_l = dl + jnp.maximum(-xl, 0.0), dl + jnp.maximum(xl, 0.0)
        east_r, west_r = dr + jnp.maximum(-xr, 0.0), dr + jnp.maximum(xr, 0.0)
        dh = jnp.where(first_half, dr, dl)
        yh = jnp.where(first_half, yr, yl)
        mh = jnp.where(first_half, mr, ml)
        east_h = jnp.where(first_half, east_r, east_l)
        west_h = jnp.where(first_half, west_r, west_l)
        from_west = (
            jnp.where(is_first, down_x(east_l), down_x(east_c)),
            jnp.where(first_half, jnp.where(is_first, down_x(east_c), down_x(east_r)), down_x(east_l)),
        )
        from_east = (
            jnp.where(is_end, up_x(west_r), up_x(west_c)),
            jnp.where(first_half, up_x(west_r), jnp.where(is_end, up_x(west_c), up_x(west_l))),
        )
        for which, (d, e, w, y, m) in enumerate(
            ((dc, east_c, west_c, yc, mc), (dh, east_h, west_h, yh, mh))
        ):
            north, south = d + jnp.maximum(-y, 0.0), d + jnp.maximum(y, 0.0)
            coef[l, which, 0] = 1.0 - (e + w + north + south + m + m)
            coef[l, which, 1] = from_west[which]
            coef[l, which, 2] = from_east[which]
            coef[l, which, 3] = jnp.where(y_of == 0, 0.0, pltpu.roll(north, 1, 1))
            coef[l, which, 4] = jnp.where(y_of == NY - 1, 0.0, pltpu.roll(south, NY - 1, 1))
            coef[l, which, 5] = m
        return carry

    lax.fori_loop(0, LEV, make_rates, 0, unroll=2)

    def relay(side):
        for i in range(OWN):
            each(side.is_relay, [side.detour[i]], arrive)
            each(side.is_relay, [side.relayed[i]], begin)

    relay(sides[0])

    @pl.when(core == 1)
    def _():
        pass_on(0, 2)

    for side in sides:
        each(side.receives, side.early, arrive)

    def halo_forcing(n, carry):
        fill_forcing(forcing, 1, n, [(nl[n], kl[pl.ds(n, 1)], 4, TX), (nr[n], kr[pl.ds(n, 1)], 0, 4)])
        return carry

    lax.fori_loop(0, STEPS_DEV, halo_forcing, 0, unroll=4)

    @pl.when(core == 1)
    def _():
        pass_on(2, DEPTH)

    @pl.when(s == 0)
    def _():
        pl.semaphore_wait(ready, 1)

    relay(sides[1])


    def next_forcing(n):
        m = n + STEPS_DEV
        fill_forcing(forcing, 0, m, [(nc[m], kc2[pl.ds(n, 1)], 0, TX)])
        fill_forcing(forcing, 1, m, [(nl[m], kl2[pl.ds(n, 1)], 4, TX), (nr[m], kr2[pl.ds(n, 1)], 0, 4)])

    def sweep(first, loads, dst, plane, last):
        def level(l):
            own_mix = coef[l, 0, 5]
            halo_mix = None if last else coef[l, 1, 5]
            found = []
            for load in loads:
                c, h = load(l)
                whole = h
                if isinstance(h, tuple):
                    whole = jnp.where(first_half, h[1], h[0])
                found.append((c, h, whole, (own_mix * c, None if last else halo_mix * whole)))
            return found

        levels = [level(0), level(1)]
        for l in range(LEV):
            if 0 < l < LEV - 1:
                levels.append(level(l + 1))
            factor = [[coef[l, which, k] for k in range(5)] for which in range(1 if last else 2)]
            for p in range(GROUP):
                c, h, whole, _ = levels[l][p]
                cd, cu = down_x(c), up_x(c)
                if isinstance(h, tuple):
                    ld, rd, lu, ru = down_x(h[0]), down_x(h[1]), up_x(h[0]), up_x(h[1])
                    hd, hu = jnp.where(first_half, rd, ld), jnp.where(first_half, ru, lu)
                else:
                    hd, hu = down_x(whole), up_x(whole)
                    ld, ru = hd, hu
                todo = [(c, jnp.where(is_first, ld, cd), jnp.where(is_end, ru, cu))]
                if not last:
                    todo.append((whole, jnp.where(is_first, cd, hd), jnp.where(is_end, cu, hu)))
                for which, (v, west, east) in enumerate(todo):
                    keep, from_west, from_east, from_south, from_north = factor[which]
                    total = forcing[plane + p, l, which] + keep * v
                    total = total + (from_west * west + from_east * east)
                    total = total + (
                        from_south * pltpu.roll(v, 1, 1) + from_north * pltpu.roll(v, NY - 1, 1)
                    )
                    for k in (l - 1, l + 1):
                        if 0 <= k < LEV:
                            total = total + levels[k][p][3][which]
                    if last:
                        ob[first + p, l] = total
                    else:
                        dst[p, l, which] = total

    def chain(group, carry):
        first = group * GROUP
        for k in range(STEPS_DEV):
            for side in sides:
                each(side.receives & (group == k // GROUP), [side.state[k]], arrive)

        @pl.when(group == (OWN + 1) // GROUP)
        def _():
            for side in sides:
                each(side.receives, side.late, arrive)

        for p in range(GROUP):

            @pl.when(first + p > OWN)
            def _(p=p):
                next_forcing(first + p - OWN - 1)

        def start(p):
            return lambda l: (ac[first + p, l], (hl[first + p, l], hr[first + p, l]))

        sweep(first, [start(p) for p in range(GROUP)], va, first + 4, False)

        @pl.when(is_last & (group == OWN // GROUP))
        def _():
            va[OWN % GROUP] = forcing[STEPS_DEV - 1]

        bufs = (va, vb)
        for k in range(2, DEPTH + 1):
            src, dst = bufs[k % 2], bufs[(k + 1) % 2]

            @pl.when(is_last & (group == (k + 2) // GROUP))
            def _(src=src, p=(k + 2) % GROUP):
                src[p, :, 0] = CIRC_ALPHA * (src[p, :, 0] - ac[OWN])
                outside = jnp.where(first_half[None], hr[OWN], hl[OWN])
                src[p, :, 1] = CIRC_ALPHA * (src[p, :, 1] - outside)

            def middle(p, src=src):
                return lambda l: (src[p, l, 0], src[p, l, 1])

            sweep(first, [middle(p) for p in range(GROUP)], dst, first + DEPTH - k, k == DEPTH)
        for p in range(GROUP):
            pltpu.make_async_copy(ob.at[first + p], out.at[first + p], local.at[7 + first + p]).start()
        return carry

    lax.fori_loop(0, STEPS_DEV // GROUP, chain, 0)

    for i in range(STEPS_DEV):
        pltpu.make_async_copy(ob.at[i], out.at[i], local.at[7 + i]).wait()
    for side in sides:
        each(side.sends, side.early + side.late + side.state[OWN:], leave)
        each(side.sends & jnp.logical_not(side.is_entry), side.state[:OWN], leave)
        each(side.is_entry, side.detour, leave)
        each(side.is_relay, side.relayed, leave)
        for half in range(2):
            mine = slice(2 * half, 2 * half + 2)
            each(side.sends & (core == half), side.rates[mine], leave)
            each(side.receives & (core == half), side.forward[mine], leave)
    for copy in up_early + up_state:
        copy.wait_send()


def body(adjoint_iterate, innovations, station_cells, diffusivity, wind_x, wind_y, vertical_mixing):
    field = (LEV, TX, NY)
    f32, i32 = jnp.float32, jnp.int32
    scratch = (
        [pltpu.VMEM((STEPS_DEV,) + field, f32)] * 3
        + [pltpu.VMEM((STEPS_DEV + 4, LEV, NY), f32)] * 3
        + [pltpu.VMEM((STEPS_DEV, NY), i32)] * 6
        + [pltpu.VMEM((4,) + field, f32)] * 3
        + [pltpu.VMEM((LEV, 2, 6, TX, NY), f32)]
        + [pltpu.VMEM((STEPS_DEV + 4, LEV, 2, TX, NY), f32)]
        + [pltpu.VMEM((GROUP, LEV, 2, TX, NY), f32)] * 2
        + [pltpu.VMEM((STEPS_DEV,) + field, f32), pltpu.VMEM((OWN,) + field, f32)]
        + [pltpu.SemaphoreType.DMA((TRANSFERS,))] * 2
        + [pltpu.SemaphoreType.DMA((7 + STEPS_DEV,)), pltpu.SemaphoreType.REGULAR]
    )
    return pl.pallas_call(
        functools.partial(kernel, lax.axis_size("tm"), lax.axis_size("space")),
        out_shape=jax.ShapeDtypeStruct((STEPS_DEV,) + field, f32),
        in_specs=[pl.BlockSpec(memory_space=pl.ANY)] * 7,
        out_specs=pl.BlockSpec(memory_space=pl.ANY),
        scratch_shapes=scratch,
        compiler_params=pltpu.CompilerParams(
            collective_id=0, has_side_effects=True, vmem_limit_bytes=62 * 2**20
        ),
        name="update",
    )(adjoint_iterate, innovations, station_cells, diffusivity, wind_x, wind_y, vertical_mixing)


def solution(mesh):
    in_specs = (
        P("tm", None, "space", None),
        P("tm", None, "space"),
        P("tm", "space"),
        P(None, "space", None),
        P(None, "space", None),
        P(None, "space", None),
        P(None, "space", None),
    )
    out_specs = P("tm", None, "space", None)
    return jax.shard_map(body, mesh=mesh, in_specs=in_specs, out_specs=out_specs, check_vma=False)
```

```python
import functools

import jax
import jax.numpy as jnp
from jax import lax
from jax.experimental import pallas as pl
from jax.experimental.pallas import tpu as pltpu
from jax.sharding import PartitionSpec as P

MESH = pl.DeviceIdType.MESH

LEV = 16
TX = 8
NY = 128
STEPS_DEV = 8
DEPTH = 5
CIRC_ALPHA = 0.1
GROUP = 2

RATES, FORWARD, INNOV, CELLS, STATE, INNOV_UP, CELLS_UP, RELAY, PER_SIDE = 0, 4, 8, 9, 10, 18, 19, 20, 23
INNOV_T, CELLS_T, STATE_T = 2 * PER_SIDE, 2 * PER_SIDE + 1, 2 * PER_SIDE + 2
TRANSFERS = STATE_T + DEPTH
OWN = STEPS_DEV - DEPTH


def fill_forcing(forcing, which, plane, parts):
    x_of = lax.broadcasted_iota(jnp.int32, (TX, NY), 0)
    y_of = lax.broadcasted_iota(jnp.int32, (NY, NY), 0)
    total = None
    for values, cells, low, high in parts:
        column = cells // NY
        row = cells % NY
        mask = (column == x_of) & (x_of >= low) & (x_of < high)
        head = values.astype(jnp.bfloat16).astype(jnp.float32)
        rest = values - head
        pieces = [
            jnp.where(mask[None], piece[:, None, :], 0.0).reshape(LEV * TX, NY).astype(jnp.bfloat16)
            for piece in (head, rest)
        ]
        hot = jnp.where(row == y_of, 1.0, 0.0).astype(jnp.bfloat16)
        part = lax.dot_general(
            jnp.concatenate(pieces, axis=1),
            jnp.concatenate([hot, hot], axis=1),
            (((1,), (1,)), ((), ())),
            preferred_element_type=jnp.float32,
        )
        total = part if total is None else total + part
    forcing[plane, :, which] = total.reshape(LEV, TX, NY)


def kernel(
    time_parts, tiles,
    a, innov, cells, dif, wx, wy, vm, out,
    ac, hl, hr, nc, nl, nr, kc, kl, kr, kc2, kl2, kr2, rc, rl, rr, coef, forcing, va, vb, ob, hold,
    send, recv, local, ready,
):
    t = lax.axis_index("tm")
    s = lax.axis_index("space")
    before = lax.rem(t + time_parts - 1, time_parts)
    after = lax.rem(t + 1, time_parts)
    core = lax.rem(t, 2)
    sibling = t + 1 - 2 * core
    mid = tiles // 2
    has_left = s > 0
    has_right = s < tiles - 1
    is_last = t == time_parts - 1
    asks, says = (t == 0) & (s == mid - 1), is_last & (s == mid - 1)

    barrier = pltpu.get_barrier_semaphore()

    def greet(device):
        pl.semaphore_signal(barrier, inc=1, device_id=device, device_id_type=MESH)

    greet((sibling, s))

    @pl.when(jnp.logical_not(says))
    def _():
        greet((after, s))

    @pl.when(asks)
    def _():
        greet((before, s))

    for here, device in (
        (has_left, s - 1),
        (has_right, s + 1),
        (s == 0, mid - 1),
        (s == 0, mid),
        (s == tiles - 1, mid - 1),
        (s == mid, tiles - 1),
    ):

        @pl.when(here)
        def _(device=device):
            greet((t, device))

    fields = (dif, wx, wy, vm)
    loads = [
        pltpu.make_async_copy(innov, nc.at[pl.ds(0, STEPS_DEV)], local.at[0]),
        pltpu.make_async_copy(cells, kc, local.at[1]),
        pltpu.make_async_copy(a.at[pl.ds(DEPTH, OWN)], ac.at[pl.ds(0, OWN)], local.at[2]),
    ] + [pltpu.make_async_copy(f, rc.at[i], local.at[3 + i]) for i, f in enumerate(fields)]
    for load in loads:
        load.start()

    def remote(number, src, dst, device, landing=None):
        return pltpu.make_async_remote_copy(
            src_ref=src, dst_ref=dst, send_sem=send.at[number],
            recv_sem=recv.at[number if landing is None else landing],
            device_id=device, device_id_type=MESH,
        )

    class Side:
        def __init__(self, base, step, first, halo, inn, cel, cel_up, rat, relay, entry, far):
            self.sends, self.receives = (has_right, has_left) if step > 0 else (has_left, has_right)
            self.zeros = (halo, inn, cel, cel_up, rat)
            to = (t, s + step)
            cols = pl.ds(first, 5)
            edge = pl.ds(4, 4) if step > 0 else pl.ds(0, 4)
            cut = [cols if i < 2 else edge for i in range(4)]
            self.rates = [
                remote(base + RATES + i, f.at[:, cut[i]], rat.at[i, :, cut[i]], to)
                for i, f in enumerate(fields)
            ]
            self.forward = [
                remote(base + FORWARD + i, rat.at[i, :, cut[i]], rat.at[i, :, cut[i]], (sibling, s), base + RATES + i)
                for i in range(4)
            ]
            self.early = [
                remote(base + CELLS, cells, cel, to),
                remote(base + INNOV, innov, inn.at[pl.ds(0, STEPS_DEV)], to),
            ]
            self.late = [
                remote(base + CELLS_UP, kc2, cel_up, to),
                remote(base + INNOV_UP, nc.at[pl.ds(STEPS_DEV, 4)], inn.at[pl.ds(STEPS_DEV, 4)], to),
            ]
            self.is_relay, self.is_entry = s == relay, s == entry
            self.state = [
                remote(base + STATE + i, a.at[i + DEPTH, :, cols], halo.at[i, :, cols], to)
                for i in range(OWN)
            ] + [
                remote(base + STATE + i, ac.at[i, :, cols], halo.at[i, :, cols], to)
                for i in range(OWN, STEPS_DEV)
            ]
            self.straight, self.far = [i for i in range(OWN) if i not in far], far
            self.detour = [
                remote(base + STATE + i, a.at[i + DEPTH, :, cols], hold.at[i, :, cols], (t, relay), base + RELAY + i)
                for i in far
            ]
            self.relayed = [
                remote(base + RELAY + i, hold.at[i, :, cols], halo.at[i, :, cols], (t, entry + step), base + STATE + i)
                for i in far
            ]

    sides = (
        Side(0, 1, 3, hl, nl, kl, kl2, rl, tiles - 1, mid - 1, (0, 1, 2)),
        Side(PER_SIDE, -1, 0, hr, nr, kr, kr2, rr, 0, mid, (0, 1, 2)),
    )
    up_early = [
        remote(CELLS_T, cells, kc2, (before, s)),
        remote(INNOV_T, innov.at[pl.ds(0, 4)], nc.at[pl.ds(STEPS_DEV, 4)], (before, s)),
    ]
    up_state = [remote(STATE_T + i, a.at[i], ac.at[OWN + i], (before, s)) for i in range(DEPTH)]

    for side in sides:

        @pl.when(jnp.logical_not(side.receives))
        def _(side=side):
            for ref in side.zeros:
                ref[...] = jnp.zeros(ref.shape, ref.dtype)

    def each(condition, copies, act):
        @pl.when(condition)
        def _():
            for copy in copies:
                act(copy)

    def begin(copy):
        copy.start()

    def arrive(copy):
        copy.wait_recv()

    def leave(copy):
        copy.wait_send()

    def number(flag):
        return flag.astype(jnp.int32)

    pl.semaphore_wait(
        barrier,
        2 + number(has_left) + number(has_right) + 2 * number(s == mid - 1) + number(s == mid)
        + number(s == tiles - 1) + number(says) - number(asks),
    )

    @pl.when(s == mid - 1)
    def _():
        pl.semaphore_signal(ready, inc=1, device_id=(t, 0), device_id_type=MESH)

    @pl.when(says)
    def _():
        pl.semaphore_signal(ready, inc=1, device_id=(after, s), device_id_type=MESH)

    each(jnp.logical_not(asks), up_early + up_state, begin)
    for side in sides:
        for half in range(2):
            each(side.sends & (core == half), side.rates[2 * half : 2 * half + 2], begin)
    for side in sides:
        each(side.sends, side.early, begin)
        each(side.is_entry, side.detour, begin)

    for load in loads:
        load.wait()
    for i in range(OWN):
        for side in sides:
            near = side.sends if i in side.straight else side.sends & jnp.logical_not(side.is_entry)
            each(near, [side.state[i]], begin)

    def own_forcing(n, carry):
        fill_forcing(forcing, 0, n, [(nc[n], kc[pl.ds(n, 1)], 0, TX)])
        return carry

    lax.fori_loop(0, STEPS_DEV, own_forcing, 0, unroll=8)

    def pass_on(first, last):
        if first == 0:
            for copy in up_early:
                copy.wait_recv()
            for side in sides:
                each(side.sends, side.late, begin)
        for i in range(first, last):
            up_state[i].wait_recv()
            for side in sides:
                each(side.sends, [side.state[OWN + i]], begin)

    def next_own_forcing(n, carry):
        m = n + STEPS_DEV
        fill_forcing(forcing, 0, m, [(nc[m], kc2[pl.ds(n, 1)], 0, TX)])
        return carry

    @pl.when(asks)
    def _():
        pl.semaphore_wait(ready, 1)
        for copy in up_early + up_state:
            copy.start()

    @pl.when(core == 0)
    def _():
        pass_on(0, DEPTH)
        lax.fori_loop(0, 4, next_own_forcing, 0, unroll=4)

    def relay(side):
        for taken, given in zip(side.detour, side.relayed):
            each(side.is_relay, [taken], arrive)
            each(side.is_relay, [given], begin)

    relay(sides[0])

    for side in sides:
        for half in range(2):
            mine = slice(2 * half, 2 * half + 2)
            each(side.receives & (core == half), side.rates[mine], arrive)
            each(side.receives & (core == half), side.forward[mine], begin)
    for side in sides:
        for half in range(2):
            other = slice(2 - 2 * half, 4 - 2 * half)
            each(side.receives & (core == half), side.rates[other], arrive)

    x_of = lax.broadcasted_iota(jnp.int32, (TX, NY), 0)
    y_of = lax.broadcasted_iota(jnp.int32, (TX, NY), 1)
    first_half = x_of < 4
    is_first, is_end = x_of == 0, x_of == TX - 1

    def down_x(v):
        return pltpu.roll(v, 1, 0)

    def up_x(v):
        return pltpu.roll(v, TX - 1, 0)

    def make_rates(l, carry):
        def own(part):
            return part[0, l], part[1, l], part[2, l], part[3, l]

        dc, xc, yc, mc = own(rc)
        dl, xl, yl, ml = own(rl)
        dr, xr, yr, mr = own(rr)
        east_c, west_c = dc + jnp.maximum(-xc, 0.0), dc + jnp.maximum(xc, 0.0)
        east_l, west_l = dl + jnp.maximum(-xl, 0.0), dl + jnp.maximum(xl, 0.0)
        east_r, west_r = dr + jnp.maximum(-xr, 0.0), dr + jnp.maximum(xr, 0.0)
        dh = jnp.where(first_half, dr, dl)
        yh = jnp.where(first_half, yr, yl)
        mh = jnp.where(first_half, mr, ml)
        east_h = jnp.where(first_half, east_r, east_l)
        west_h = jnp.where(first_half, west_r, west_l)
        from_west = (
            jnp.where(is_first, down_x(east_l), down_x(east_c)),
            jnp.where(first_half, jnp.where(is_first, down_x(east_c), down_x(east_r)), down_x(east_l)),
        )
        from_east = (
            jnp.where(is_end, up_x(west_r), up_x(west_c)),
            jnp.where(first_half, up_x(west_r), jnp.where(is_end, up_x(west_c), up_x(west_l))),
        )
        for which, (d, e, w, y, m) in enumerate(
            ((dc, east_c, west_c, yc, mc), (dh, east_h, west_h, yh, mh))
        ):
            north, south = d + jnp.maximum(-y, 0.0), d + jnp.maximum(y, 0.0)
            coef[l, which, 0] = 1.0 - (e + w + north + south + m + m)
            coef[l, which, 1] = from_west[which]
            coef[l, which, 2] = from_east[which]
            coef[l, which, 3] = jnp.where(y_of == 0, 0.0, pltpu.roll(north, 1, 1))
            coef[l, which, 4] = jnp.where(y_of == NY - 1, 0.0, pltpu.roll(south, NY - 1, 1))
            coef[l, which, 5] = m
        return carry

    lax.fori_loop(0, LEV, make_rates, 0, unroll=2)

    @pl.when(core == 1)
    def _():
        pass_on(0, 2)
        lax.fori_loop(0, 4, next_own_forcing, 0, unroll=4)

    for side in sides:
        each(side.receives, side.early, arrive)

    def halo_forcing(n, carry):
        fill_forcing(forcing, 1, n, [(nl[n], kl[pl.ds(n, 1)], 4, TX), (nr[n], kr[pl.ds(n, 1)], 0, 4)])
        return carry

    lax.fori_loop(0, STEPS_DEV, halo_forcing, 0, unroll=8)

    @pl.when(core == 1)
    def _():
        pass_on(2, DEPTH)

    @pl.when(s == 0)
    def _():
        pl.semaphore_wait(ready, 1)

    relay(sides[1])


    def next_forcing(n, carry):
        m = n + STEPS_DEV
        fill_forcing(forcing, 1, m, [(nl[m], kl2[pl.ds(n, 1)], 4, TX), (nr[m], kr2[pl.ds(n, 1)], 0, 4)])
        return carry

    def sweep(first, loads, dst, plane, last):
        def level(l):
            own_mix = coef[l, 0, 5]
            halo_mix = None if last else coef[l, 1, 5]
            found = []
            for load in loads:
                c, h = load(l)
                whole = h
                if isinstance(h, tuple):
                    whole = jnp.where(first_half, h[1], h[0])
                found.append((c, h, whole, (own_mix * c, None if last else halo_mix * whole)))
            return found

        levels = [level(0), level(1)]
        for l in range(LEV):
            if 0 < l < LEV - 1:
                levels.append(level(l + 1))
            factor = [[coef[l, which, k] for k in range(5)] for which in range(1 if last else 2)]
            for p in range(GROUP):
                c, h, whole, _ = levels[l][p]
                cd, cu = down_x(c), up_x(c)
                if isinstance(h, tuple):
                    ld, rd, lu, ru = down_x(h[0]), down_x(h[1]), up_x(h[0]), up_x(h[1])
                    hd, hu = jnp.where(first_half, rd, ld), jnp.where(first_half, ru, lu)
                else:
                    hd, hu = down_x(whole), up_x(whole)
                    ld, ru = hd, hu
                todo = [(c, jnp.where(is_first, ld, cd), jnp.where(is_end, ru, cu))]
                if not last:
                    todo.append((whole, jnp.where(is_first, cd, hd), jnp.where(is_end, cu, hu)))
                for which, (v, west, east) in enumerate(todo):
                    keep, from_west, from_east, from_south, from_north = factor[which]
                    total = forcing[plane + p, l, which] + keep * v
                    total = total + (from_west * west + from_east * east)
                    total = total + (
                        from_south * pltpu.roll(v, 1, 1) + from_north * pltpu.roll(v, NY - 1, 1)
                    )
                    for k in (l - 1, l + 1):
                        if 0 <= k < LEV:
                            total = total + levels[k][p][3][which]
                    if last:
                        ob[first + p, l] = total
                    else:
                        dst[p, l, which] = total

    def chain(group, carry):
        first = group * GROUP
        for k in range(STEPS_DEV):
            for side in sides:
                each(side.receives & (group == k // GROUP), [side.state[k]], arrive)

        @pl.when(group == (OWN + 1) // GROUP)
        def _():
            for side in sides:
                each(side.receives, side.late, arrive)
            lax.fori_loop(0, 4, next_forcing, 0, unroll=4)

        def start(p):
            return lambda l: (ac[first + p, l], (hl[first + p, l], hr[first + p, l]))

        sweep(first, [start(p) for p in range(GROUP)], va, first + 4, False)

        @pl.when(is_last & (group == OWN // GROUP))
        def _():
            va[OWN % GROUP] = forcing[STEPS_DEV - 1]

        bufs = (va, vb)
        for k in range(2, DEPTH + 1):
            src, dst = bufs[k % 2], bufs[(k + 1) % 2]

            @pl.when(is_last & (group == (k + 2) // GROUP))
            def _(src=src, p=(k + 2) % GROUP):
                src[p, :, 0] = CIRC_ALPHA * (src[p, :, 0] - ac[OWN])
                outside = jnp.where(first_half[None], hr[OWN], hl[OWN])
                src[p, :, 1] = CIRC_ALPHA * (src[p, :, 1] - outside)

            def middle(p, src=src):
                return lambda l: (src[p, l, 0], src[p, l, 1])

            sweep(first, [middle(p) for p in range(GROUP)], dst, first + DEPTH - k, k == DEPTH)
        for p in range(GROUP):
            pltpu.make_async_copy(ob.at[first + p], out.at[first + p], local.at[7 + first + p]).start()
        return carry

    lax.fori_loop(0, STEPS_DEV // GROUP, chain, 0)

    for i in range(STEPS_DEV):
        pltpu.make_async_copy(ob.at[i], out.at[i], local.at[7 + i]).wait()
    for side in sides:
        each(side.sends, side.early + side.late + side.state[OWN:], leave)
        each(side.sends, [side.state[i] for i in side.straight], leave)
        each(side.sends & jnp.logical_not(side.is_entry), [side.state[i] for i in side.far], leave)
        each(side.is_entry, side.detour, leave)
        each(side.is_relay, side.relayed, leave)
        for half in range(2):
            mine = slice(2 * half, 2 * half + 2)
            each(side.sends & (core == half), side.rates[mine], leave)
            each(side.receives & (core == half), side.forward[mine], leave)
    for copy in up_early + up_state:
        copy.wait_send()


def body(adjoint_iterate, innovations, station_cells, diffusivity, wind_x, wind_y, vertical_mixing):
    field = (LEV, TX, NY)
    f32, i32 = jnp.float32, jnp.int32
    scratch = (
        [pltpu.VMEM((STEPS_DEV,) + field, f32)] * 3
        + [pltpu.VMEM((STEPS_DEV + 4, LEV, NY), f32)] * 3
        + [pltpu.VMEM((STEPS_DEV, NY), i32)] * 6
        + [pltpu.VMEM((4,) + field, f32)] * 3
        + [pltpu.VMEM((LEV, 2, 6, TX, NY), f32)]
        + [pltpu.VMEM((STEPS_DEV + 4, LEV, 2, TX, NY), f32)]
        + [pltpu.VMEM((GROUP, LEV, 2, TX, NY), f32)] * 2
        + [pltpu.VMEM((STEPS_DEV,) + field, f32), pltpu.VMEM((OWN,) + field, f32)]
        + [pltpu.SemaphoreType.DMA((TRANSFERS,))] * 2
        + [pltpu.SemaphoreType.DMA((7 + STEPS_DEV,)), pltpu.SemaphoreType.REGULAR]
    )
    return pl.pallas_call(
        functools.partial(kernel, lax.axis_size("tm"), lax.axis_size("space")),
        out_shape=jax.ShapeDtypeStruct((STEPS_DEV,) + field, f32),
        in_specs=[pl.BlockSpec(memory_space=pl.ANY)] * 7,
        out_specs=pl.BlockSpec(memory_space=pl.ANY),
        scratch_shapes=scratch,
        compiler_params=pltpu.CompilerParams(
            collective_id=0, has_side_effects=True, vmem_limit_bytes=62 * 2**20
        ),
        name="update",
    )(adjoint_iterate, innovations, station_cells, diffusivity, wind_x, wind_y, vertical_mixing)


def solution(mesh):
    in_specs = (
        P("tm", None, "space", None),
        P("tm", None, "space"),
        P("tm", "space"),
        P(None, "space", None),
        P(None, "space", None),
        P(None, "space", None),
        P(None, "space", None),
    )
    out_specs = P("tm", None, "space", None)
    return jax.shard_map(body, mesh=mesh, in_specs=in_specs, out_specs=out_specs, check_vma=False)
```

```python
import functools

import jax
import jax.numpy as jnp
from jax import lax
from jax.experimental import pallas as pl
from jax.experimental.pallas import tpu as pltpu
from jax.sharding import PartitionSpec as P

MESH = pl.DeviceIdType.MESH

LEV = 16
TX = 8
NY = 128
STEPS_DEV = 8
DEPTH = 5
CIRC_ALPHA = 0.1
GROUP = 2

RATES, FORWARD, INNOV, CELLS, STATE, INNOV_UP, CELLS_UP, RELAY, PER_SIDE = 0, 4, 8, 9, 10, 18, 19, 20, 23
INNOV_T, CELLS_T, STATE_T = 2 * PER_SIDE, 2 * PER_SIDE + 1, 2 * PER_SIDE + 2
TRANSFERS = STATE_T + DEPTH
OWN = STEPS_DEV - DEPTH


def fill_forcing(forcing, which, plane, parts):
    x_of = lax.broadcasted_iota(jnp.int32, (TX, NY), 0)
    y_of = lax.broadcasted_iota(jnp.int32, (NY, NY), 0)
    total = None
    for values, cells, low, high in parts:
        column = cells // NY
        row = cells % NY
        mask = (column == x_of) & (x_of >= low) & (x_of < high)
        head = values.astype(jnp.bfloat16).astype(jnp.float32)
        rest = values - head
        pieces = [
            jnp.where(mask[None], piece[:, None, :], 0.0).reshape(LEV * TX, NY).astype(jnp.bfloat16)
            for piece in (head, rest)
        ]
        hot = jnp.where(row == y_of, 1.0, 0.0).astype(jnp.bfloat16)
        part = lax.dot_general(
            jnp.concatenate(pieces, axis=1),
            jnp.concatenate([hot, hot], axis=1),
            (((1,), (1,)), ((), ())),
            preferred_element_type=jnp.float32,
        )
        total = part if total is None else total + part
    forcing[plane, :, which] = total.reshape(LEV, TX, NY)


def kernel(
    time_parts, tiles,
    a, innov, cells, dif, wx, wy, vm, out,
    ac, hl, hr, nc, nl, nr, kc, kl, kr, kc2, kl2, kr2, rc, rl, rr, coef, forcing, va, vb, hold,
    send, recv, local, ready,
):
    t = lax.axis_index("tm")
    s = lax.axis_index("space")
    before = lax.rem(t + time_parts - 1, time_parts)
    after = lax.rem(t + 1, time_parts)
    core = lax.rem(t, 2)
    sibling = t + 1 - 2 * core
    mid = tiles // 2
    has_left = s > 0
    has_right = s < tiles - 1
    is_last = t == time_parts - 1
    asks, says = (t == 0) & (s == mid - 1), is_last & (s == mid - 1)

    barrier = pltpu.get_barrier_semaphore()

    def greet(device):
        pl.semaphore_signal(barrier, inc=1, device_id=device, device_id_type=MESH)

    greet((sibling, s))

    @pl.when(jnp.logical_not(says))
    def _():
        greet((after, s))

    @pl.when(asks)
    def _():
        greet((before, s))

    for here, device in (
        (has_left, s - 1),
        (has_right, s + 1),
        (s == 0, mid - 1),
        (s == 0, mid),
        (s == tiles - 1, mid - 1),
        (s == mid, tiles - 1),
    ):

        @pl.when(here)
        def _(device=device):
            greet((t, device))

    fields = (dif, wx, wy, vm)
    loads = [
        pltpu.make_async_copy(innov, nc.at[pl.ds(0, STEPS_DEV)], local.at[0]),
        pltpu.make_async_copy(cells, kc, local.at[1]),
        pltpu.make_async_copy(a.at[pl.ds(DEPTH, OWN)], ac.at[pl.ds(0, OWN)], local.at[2]),
    ] + [pltpu.make_async_copy(f, rc.at[i], local.at[3 + i]) for i, f in enumerate(fields)]
    for load in loads:
        load.start()

    def remote(number, src, dst, device, landing=None):
        return pltpu.make_async_remote_copy(
            src_ref=src, dst_ref=dst, send_sem=send.at[number],
            recv_sem=recv.at[number if landing is None else landing],
            device_id=device, device_id_type=MESH,
        )

    class Side:
        def __init__(self, base, step, first, halo, inn, cel, cel_up, rat, relay, entry, far):
            self.sends, self.receives = (has_right, has_left) if step > 0 else (has_left, has_right)
            self.zeros = (halo, inn, cel, cel_up, rat)
            to = (t, s + step)
            cols = pl.ds(first, 5)
            edge = pl.ds(4, 4) if step > 0 else pl.ds(0, 4)
            cut = [cols if i < 2 else edge for i in range(4)]
            self.rates = [
                remote(base + RATES + i, f.at[:, cut[i]], rat.at[i, :, cut[i]], to)
                for i, f in enumerate(fields)
            ]
            self.forward = [
                remote(base + FORWARD + i, rat.at[i, :, cut[i]], rat.at[i, :, cut[i]], (sibling, s), base + RATES + i)
                for i in range(4)
            ]
            self.early = [
                remote(base + CELLS, cells, cel, to),
                remote(base + INNOV, innov, inn.at[pl.ds(0, STEPS_DEV)], to),
            ]
            self.late = [
                remote(base + CELLS_UP, kc2, cel_up, to),
                remote(base + INNOV_UP, nc.at[pl.ds(STEPS_DEV, 4)], inn.at[pl.ds(STEPS_DEV, 4)], to),
            ]
            self.is_relay, self.is_entry = s == relay, s == entry
            self.state = [
                remote(base + STATE + i, a.at[i + DEPTH, :, cols], halo.at[i, :, cols], to)
                for i in range(OWN)
            ] + [
                remote(base + STATE + i, ac.at[i, :, cols], halo.at[i, :, cols], to)
                for i in range(OWN, STEPS_DEV)
            ]
            self.straight, self.far = [i for i in range(OWN) if i not in far], far
            self.detour = [
                remote(base + STATE + i, a.at[i + DEPTH, :, cols], hold.at[i, :, cols], (t, relay), base + RELAY + i)
                for i in far
            ]
            self.relayed = [
                remote(base + RELAY + i, hold.at[i, :, cols], halo.at[i, :, cols], (t, entry + step), base + STATE + i)
                for i in far
            ]

    sides = (
        Side(0, 1, 3, hl, nl, kl, kl2, rl, tiles - 1, mid - 1, (0, 1, 2)),
        Side(PER_SIDE, -1, 0, hr, nr, kr, kr2, rr, 0, mid, (0, 1, 2)),
    )
    up_early = [
        remote(CELLS_T, cells, kc2, (before, s)),
        remote(INNOV_T, innov.at[pl.ds(0, 4)], nc.at[pl.ds(STEPS_DEV, 4)], (before, s)),
    ]
    up_state = [remote(STATE_T + i, a.at[i], ac.at[OWN + i], (before, s)) for i in range(DEPTH)]

    for side in sides:

        @pl.when(jnp.logical_not(side.receives))
        def _(side=side):
            for ref in side.zeros:
                ref[...] = jnp.zeros(ref.shape, ref.dtype)

    def each(condition, copies, act):
        @pl.when(condition)
        def _():
            for copy in copies:
                act(copy)

    def begin(copy):
        copy.start()

    def arrive(copy):
        copy.wait_recv()

    def leave(copy):
        copy.wait_send()

    def number(flag):
        return flag.astype(jnp.int32)

    pl.semaphore_wait(
        barrier,
        2 + number(has_left) + number(has_right) + 2 * number(s == mid - 1) + number(s == mid)
        + number(s == tiles - 1) + number(says) - number(asks),
    )

    @pl.when(s == mid - 1)
    def _():
        pl.semaphore_signal(ready, inc=1, device_id=(t, 0), device_id_type=MESH)

    @pl.when(says)
    def _():
        pl.semaphore_signal(ready, inc=1, device_id=(after, s), device_id_type=MESH)

    each(jnp.logical_not(asks), up_early + up_state, begin)
    for side in sides:
        for half in range(2):
            each(side.sends & (core == half), side.rates[2 * half : 2 * half + 2], begin)
    for side in sides:
        each(side.sends, side.early, begin)
        each(side.is_entry, side.detour, begin)

    for load in loads:
        load.wait()
    for i in range(OWN):
        for side in sides:
            near = side.sends if i in side.straight else side.sends & jnp.logical_not(side.is_entry)
            each(near, [side.state[i]], begin)

    def own_forcing(n, carry):
        fill_forcing(forcing, 0, n, [(nc[n], kc[pl.ds(n, 1)], 0, TX)])
        return carry

    lax.fori_loop(0, STEPS_DEV, own_forcing, 0, unroll=8)

    def pass_on(first, last):
        if first == 0:
            for copy in up_early:
                copy.wait_recv()
            for side in sides:
                each(side.sends, side.late, begin)
        for i in range(first, last):
            up_state[i].wait_recv()
            for side in sides:
                each(side.sends, [side.state[OWN + i]], begin)

    def next_own_forcing(n, carry):
        m = n + STEPS_DEV
        fill_forcing(forcing, 0, m, [(nc[m], kc2[pl.ds(n, 1)], 0, TX)])
        return carry

    @pl.when(asks)
    def _():
        pl.semaphore_wait(ready, 1)
        for copy in up_early + up_state:
            copy.start()

    @pl.when(core == 0)
    def _():
        pass_on(0, DEPTH)
        lax.fori_loop(0, 4, next_own_forcing, 0, unroll=4)

    def relay(side):
        for taken, given in zip(side.detour, side.relayed):
            each(side.is_relay, [taken], arrive)
            each(side.is_relay, [given], begin)

    relay(sides[0])

    for side in sides:
        for half in range(2):
            mine = slice(2 * half, 2 * half + 2)
            each(side.receives & (core == half), side.rates[mine], arrive)
            each(side.receives & (core == half), side.forward[mine], begin)
    for side in sides:
        for half in range(2):
            other = slice(2 - 2 * half, 4 - 2 * half)
            each(side.receives & (core == half), side.rates[other], arrive)

    x_of = lax.broadcasted_iota(jnp.int32, (TX, NY), 0)
    y_of = lax.broadcasted_iota(jnp.int32, (TX, NY), 1)
    first_half = x_of < 4
    is_first, is_end = x_of == 0, x_of == TX - 1

    def down_x(v):
        return pltpu.roll(v, 1, 0)

    def up_x(v):
        return pltpu.roll(v, TX - 1, 0)

    def make_rates(l, carry):
        def own(part):
            return part[0, l], part[1, l], part[2, l], part[3, l]

        dc, xc, yc, mc = own(rc)
        dl, xl, yl, ml = own(rl)
        dr, xr, yr, mr = own(rr)
        east_c, west_c = dc + jnp.maximum(-xc, 0.0), dc + jnp.maximum(xc, 0.0)
        east_l, west_l = dl + jnp.maximum(-xl, 0.0), dl + jnp.maximum(xl, 0.0)
        east_r, west_r = dr + jnp.maximum(-xr, 0.0), dr + jnp.maximum(xr, 0.0)
        dh = jnp.where(first_half, dr, dl)
        yh = jnp.where(first_half, yr, yl)
        mh = jnp.where(first_half, mr, ml)
        east_h = jnp.where(first_half, east_r, east_l)
        west_h = jnp.where(first_half, west_r, west_l)
        from_west = (
            jnp.where(is_first, down_x(east_l), down_x(east_c)),
            jnp.where(first_half, jnp.where(is_first, down_x(east_c), down_x(east_r)), down_x(east_l)),
        )
        from_east = (
            jnp.where(is_end, up_x(west_r), up_x(west_c)),
            jnp.where(first_half, up_x(west_r), jnp.where(is_end, up_x(west_c), up_x(west_l))),
        )
        for which, (d, e, w, y, m) in enumerate(
            ((dc, east_c, west_c, yc, mc), (dh, east_h, west_h, yh, mh))
        ):
            north, south = d + jnp.maximum(-y, 0.0), d + jnp.maximum(y, 0.0)
            coef[l, which, 0] = 1.0 - (e + w + north + south + m + m)
            coef[l, which, 1] = from_west[which]
            coef[l, which, 2] = from_east[which]
            coef[l, which, 3] = jnp.where(y_of == 0, 0.0, pltpu.roll(north, 1, 1))
            coef[l, which, 4] = jnp.where(y_of == NY - 1, 0.0, pltpu.roll(south, NY - 1, 1))
            coef[l, which, 5] = m
        return carry

    lax.fori_loop(0, LEV, make_rates, 0, unroll=2)

    @pl.when(core == 1)
    def _():
        pass_on(0, 2)
        lax.fori_loop(0, 4, next_own_forcing, 0, unroll=4)

    for side in sides:
        each(side.receives, side.early, arrive)

    def halo_forcing(n, carry):
        fill_forcing(forcing, 1, n, [(nl[n], kl[pl.ds(n, 1)], 4, TX), (nr[n], kr[pl.ds(n, 1)], 0, 4)])
        return carry

    lax.fori_loop(0, STEPS_DEV, halo_forcing, 0, unroll=8)

    @pl.when(core == 1)
    def _():
        pass_on(2, DEPTH)

    @pl.when(s == 0)
    def _():
        pl.semaphore_wait(ready, 1)

    relay(sides[1])


    def next_forcing(n, carry):
        m = n + STEPS_DEV
        fill_forcing(forcing, 1, m, [(nl[m], kl2[pl.ds(n, 1)], 4, TX), (nr[m], kr2[pl.ds(n, 1)], 0, 4)])
        return carry

    def sweep(first, loads, dst, plane, last):
        def level(l):
            own_mix = coef[l, 0, 5]
            halo_mix = None if last else coef[l, 1, 5]
            found = []
            for load in loads:
                c, h = load(l)
                whole = h
                if isinstance(h, tuple):
                    whole = jnp.where(first_half, h[1], h[0])
                found.append((c, h, whole, (own_mix * c, None if last else halo_mix * whole)))
            return found

        levels = [level(0), level(1)]
        for l in range(LEV):
            if 0 < l < LEV - 1:
                levels.append(level(l + 1))
            factor = [[coef[l, which, k] for k in range(5)] for which in range(1 if last else 2)]
            for p in range(GROUP):
                c, h, whole, _ = levels[l][p]
                cd, cu = down_x(c), up_x(c)
                if isinstance(h, tuple):
                    ld, rd, lu, ru = down_x(h[0]), down_x(h[1]), up_x(h[0]), up_x(h[1])
                    hd, hu = jnp.where(first_half, rd, ld), jnp.where(first_half, ru, lu)
                else:
                    hd, hu = down_x(whole), up_x(whole)
                    ld, ru = hd, hu
                todo = [(c, jnp.where(is_first, ld, cd), jnp.where(is_end, ru, cu))]
                if not last:
                    todo.append((whole, jnp.where(is_first, cd, hd), jnp.where(is_end, cu, hu)))
                for which, (v, west, east) in enumerate(todo):
                    keep, from_west, from_east, from_south, from_north = factor[which]
                    total = forcing[plane + p, l, which] + keep * v
                    total = total + (from_west * west + from_east * east)
                    total = total + (
                        from_south * pltpu.roll(v, 1, 1) + from_north * pltpu.roll(v, NY - 1, 1)
                    )
                    for k in (l - 1, l + 1):
                        if 0 <= k < LEV:
                            total = total + levels[k][p][3][which]
                    if last:
                        out[first + p, l] = total
                    else:
                        dst[p, l, which] = total

    def chain(group, carry):
        first = group * GROUP
        for k in range(STEPS_DEV):
            for side in sides:
                each(side.receives & (group == k // GROUP), [side.state[k]], arrive)

        @pl.when(group == (OWN + 1) // GROUP)
        def _():
            for side in sides:
                each(side.receives, side.late, arrive)
            lax.fori_loop(0, 4, next_forcing, 0, unroll=4)

        def start(p):
            return lambda l: (ac[first + p, l], (hl[first + p, l], hr[first + p, l]))

        sweep(first, [start(p) for p in range(GROUP)], va, first + 4, False)

        @pl.when(is_last & (group == OWN // GROUP))
        def _():
            va[OWN % GROUP] = forcing[STEPS_DEV - 1]

        bufs = (va, vb)
        for k in range(2, DEPTH + 1):
            src, dst = bufs[k % 2], bufs[(k + 1) % 2]

            @pl.when(is_last & (group == (k + 2) // GROUP))
            def _(src=src, p=(k + 2) % GROUP):
                src[p, :, 0] = CIRC_ALPHA * (src[p, :, 0] - ac[OWN])
                outside = jnp.where(first_half[None], hr[OWN], hl[OWN])
                src[p, :, 1] = CIRC_ALPHA * (src[p, :, 1] - outside)

            def middle(p, src=src):
                return lambda l: (src[p, l, 0], src[p, l, 1])

            sweep(first, [middle(p) for p in range(GROUP)], dst, first + DEPTH - k, k == DEPTH)
        return carry

    lax.fori_loop(0, STEPS_DEV // GROUP, chain, 0)

    for side in sides:
        each(side.sends, side.early + side.late + side.state[OWN:], leave)
        each(side.sends, [side.state[i] for i in side.straight], leave)
        each(side.sends & jnp.logical_not(side.is_entry), [side.state[i] for i in side.far], leave)
        each(side.is_entry, side.detour, leave)
        each(side.is_relay, side.relayed, leave)
        for half in range(2):
            mine = slice(2 * half, 2 * half + 2)
            each(side.sends & (core == half), side.rates[mine], leave)
            each(side.receives & (core == half), side.forward[mine], leave)
    for copy in up_early + up_state:
        copy.wait_send()


def body(adjoint_iterate, innovations, station_cells, diffusivity, wind_x, wind_y, vertical_mixing):
    field = (LEV, TX, NY)
    f32, i32 = jnp.float32, jnp.int32
    scratch = (
        [pltpu.VMEM((STEPS_DEV,) + field, f32)] * 3
        + [pltpu.VMEM((STEPS_DEV + 4, LEV, NY), f32)] * 3
        + [pltpu.VMEM((STEPS_DEV, NY), i32)] * 6
        + [pltpu.VMEM((4,) + field, f32)] * 3
        + [pltpu.VMEM((LEV, 2, 6, TX, NY), f32)]
        + [pltpu.VMEM((STEPS_DEV + 4, LEV, 2, TX, NY), f32)]
        + [pltpu.VMEM((GROUP, LEV, 2, TX, NY), f32)] * 2
        + [pltpu.VMEM((OWN,) + field, f32)]
        + [pltpu.SemaphoreType.DMA((TRANSFERS,))] * 2
        + [pltpu.SemaphoreType.DMA((7,)), pltpu.SemaphoreType.REGULAR]
    )
    return pl.pallas_call(
        functools.partial(kernel, lax.axis_size("tm"), lax.axis_size("space")),
        out_shape=jax.ShapeDtypeStruct((STEPS_DEV,) + field, f32),
        in_specs=[pl.BlockSpec(memory_space=pl.ANY)] * 7,
        out_specs=pl.BlockSpec(memory_space=pltpu.VMEM),
        scratch_shapes=scratch,
        compiler_params=pltpu.CompilerParams(
            collective_id=0, has_side_effects=True, vmem_limit_bytes=24 * 2**20
        ),
        name="update",
    )(*[
        pltpu.with_memory_space_constraint(x, pltpu.HBM)
        for x in (adjoint_iterate, innovations, station_cells, diffusivity, wind_x, wind_y, vertical_mixing)
    ])


def solution(mesh):
    in_specs = (
        P("tm", None, "space", None),
        P("tm", None, "space"),
        P("tm", "space"),
        P(None, "space", None),
        P(None, "space", None),
        P(None, "space", None),
        P(None, "space", None),
    )
    out_specs = P("tm", None, "space", None)
    return jax.shard_map(body, mesh=mesh, in_specs=in_specs, out_specs=out_specs, check_vma=False)
```

```python
import functools

import jax
import jax.numpy as jnp
from jax import lax
from jax.experimental import pallas as pl
from jax.experimental.pallas import tpu as pltpu
from jax.sharding import PartitionSpec as P

MESH = pl.DeviceIdType.MESH

LEV = 16
TX = 8
NY = 128
STEPS_DEV = 8
DEPTH = 5
CIRC_ALPHA = 0.1
GROUP = 2

RATES, FORWARD, INNOV, CELLS, STATE, INNOV_UP, CELLS_UP, RELAY, PER_SIDE = 0, 4, 8, 9, 10, 18, 19, 20, 23
INNOV_T, CELLS_T, STATE_T = 2 * PER_SIDE, 2 * PER_SIDE + 1, 2 * PER_SIDE + 2
TRANSFERS = STATE_T + DEPTH
OWN = STEPS_DEV - DEPTH


def fill_forcing(forcing, which, plane, parts):
    x_of = lax.broadcasted_iota(jnp.int32, (TX, NY), 0)
    y_of = lax.broadcasted_iota(jnp.int32, (NY, NY), 0)
    total = None
    for values, cells, low, high in parts:
        column = cells // NY
        row = cells % NY
        mask = (column == x_of) & (x_of >= low) & (x_of < high)
        head = values.astype(jnp.bfloat16).astype(jnp.float32)
        rest = values - head
        pieces = [
            jnp.where(mask[None], piece[:, None, :], 0.0).reshape(LEV * TX, NY).astype(jnp.bfloat16)
            for piece in (head, rest)
        ]
        hot = jnp.where(row == y_of, 1.0, 0.0).astype(jnp.bfloat16)
        part = lax.dot_general(
            jnp.concatenate(pieces, axis=1),
            jnp.concatenate([hot, hot], axis=1),
            (((1,), (1,)), ((), ())),
            preferred_element_type=jnp.float32,
        )
        total = part if total is None else total + part
    forcing[plane, :, which] = total.reshape(LEV, TX, NY)


def kernel(
    time_parts, tiles,
    a, innov, cells, dif, wx, wy, vm, out,
    ac, hl, hr, nc, nl, nr, kc, kl, kr, kc2, kl2, kr2, rc, rl, rr, coef, forcing, va, vb, hold,
    send, recv, local, ready,
):
    t = lax.axis_index("tm")
    s = lax.axis_index("space")
    before = lax.rem(t + time_parts - 1, time_parts)
    after = lax.rem(t + 1, time_parts)
    core = lax.rem(t, 2)
    sibling = t + 1 - 2 * core
    mid = tiles // 2
    has_left = s > 0
    has_right = s < tiles - 1
    is_last = t == time_parts - 1
    asks, says = (core == 0) & (s == mid - 1), (core == 1) & (s == mid - 1)

    barrier = pltpu.get_barrier_semaphore()

    def greet(device):
        pl.semaphore_signal(barrier, inc=1, device_id=device, device_id_type=MESH)

    greet((sibling, s))

    @pl.when(jnp.logical_not(says))
    def _():
        greet((after, s))

    @pl.when(asks)
    def _():
        greet((before, s))

    for here, device in (
        (has_left, s - 1),
        (has_right, s + 1),
        (s == 0, mid - 1),
        (s == 0, mid),
        (s == tiles - 1, mid - 1),
        (s == mid, tiles - 1),
    ):

        @pl.when(here)
        def _(device=device):
            greet((t, device))

    fields = (dif, wx, wy, vm)
    loads = [
        pltpu.make_async_copy(innov, nc.at[pl.ds(0, STEPS_DEV)], local.at[0]),
        pltpu.make_async_copy(cells, kc, local.at[1]),
        pltpu.make_async_copy(a.at[pl.ds(DEPTH, OWN)], ac.at[pl.ds(0, OWN)], local.at[2]),
    ] + [pltpu.make_async_copy(f, rc.at[i], local.at[3 + i]) for i, f in enumerate(fields)]
    for load in loads:
        load.start()

    def remote(number, src, dst, device, landing=None):
        return pltpu.make_async_remote_copy(
            src_ref=src, dst_ref=dst, send_sem=send.at[number],
            recv_sem=recv.at[number if landing is None else landing],
            device_id=device, device_id_type=MESH,
        )

    class Side:
        def __init__(self, base, step, first, halo, inn, cel, cel_up, rat, relay, entry, far):
            self.sends, self.receives = (has_right, has_left) if step > 0 else (has_left, has_right)
            self.zeros = (halo, inn, cel, cel_up, rat)
            to = (t, s + step)
            cols = pl.ds(first, 5)
            edge = pl.ds(4, 4) if step > 0 else pl.ds(0, 4)
            cut = [cols if i < 2 else edge for i in range(4)]
            self.rates = [
                remote(base + RATES + i, f.at[:, cut[i]], rat.at[i, :, cut[i]], to)
                for i, f in enumerate(fields)
            ]
            self.forward = [
                remote(base + FORWARD + i, rat.at[i, :, cut[i]], rat.at[i, :, cut[i]], (sibling, s), base + RATES + i)
                for i in range(4)
            ]
            self.early = [
                remote(base + CELLS, cells, cel, to),
                remote(base + INNOV, innov, inn.at[pl.ds(0, STEPS_DEV)], to),
            ]
            self.late = [
                remote(base + CELLS_UP, kc2, cel_up, to),
                remote(base + INNOV_UP, nc.at[pl.ds(STEPS_DEV, 4)], inn.at[pl.ds(STEPS_DEV, 4)], to),
            ]
            self.is_relay, self.is_entry = s == relay, s == entry
            self.state = [
                remote(base + STATE + i, a.at[i + DEPTH, :, cols], halo.at[i, :, cols], to)
                for i in range(OWN)
            ] + [
                remote(base + STATE + i, ac.at[i, :, cols], halo.at[i, :, cols], to)
                for i in range(OWN, STEPS_DEV)
            ]
            self.straight, self.far = [i for i in range(OWN) if i not in far], far
            self.detour = [
                remote(base + STATE + i, a.at[i + DEPTH, :, cols], hold.at[i, :, cols], (t, relay), base + RELAY + i)
                for i in far
            ]
            self.relayed = [
                remote(base + RELAY + i, hold.at[i, :, cols], halo.at[i, :, cols], (t, entry + step), base + STATE + i)
                for i in far
            ]

    sides = (
        Side(0, 1, 3, hl, nl, kl, kl2, rl, tiles - 1, mid - 1, (0, 1, 2)),
        Side(PER_SIDE, -1, 0, hr, nr, kr, kr2, rr, 0, mid, (0, 1, 2)),
    )
    up_early = [
        remote(CELLS_T, cells, kc2, (before, s)),
        remote(INNOV_T, innov.at[pl.ds(0, 4)], nc.at[pl.ds(STEPS_DEV, 4)], (before, s)),
    ]
    up_state = [remote(STATE_T + i, a.at[i], ac.at[OWN + i], (before, s)) for i in range(DEPTH)]

    for side in sides:

        @pl.when(jnp.logical_not(side.receives))
        def _(side=side):
            for ref in side.zeros:
                ref[...] = jnp.zeros(ref.shape, ref.dtype)

    def each(condition, copies, act):
        @pl.when(condition)
        def _():
            for copy in copies:
                act(copy)

    def begin(copy):
        copy.start()

    def arrive(copy):
        copy.wait_recv()

    def leave(copy):
        copy.wait_send()

    def number(flag):
        return flag.astype(jnp.int32)

    pl.semaphore_wait(
        barrier,
        2 + number(has_left) + number(has_right) + 2 * number(s == mid - 1) + number(s == mid)
        + number(s == tiles - 1) + number(says) - number(asks),
    )

    @pl.when(s == mid - 1)
    def _():
        pl.semaphore_signal(ready, inc=1, device_id=(t, 0), device_id_type=MESH)

    @pl.when(says)
    def _():
        pl.semaphore_signal(ready, inc=1, device_id=(after, s), device_id_type=MESH)

    each(jnp.logical_not(asks), up_early + up_state, begin)
    for side in sides:
        for half in range(2):
            each(side.sends & (core == half), side.rates[2 * half : 2 * half + 2], begin)
    for side in sides:
        each(side.sends if side is sides[0] else side.sends & (s != mid), side.early, begin)
        each(side.is_entry, side.detour, begin)

    for load in loads:
        load.wait()
    for i in range(OWN):
        for side in sides:
            near = side.sends if i in side.straight else side.sends & jnp.logical_not(side.is_entry)
            each(near, [side.state[i]], begin)

    def own_forcing(n, carry):
        fill_forcing(forcing, 0, n, [(nc[n], kc[pl.ds(n, 1)], 0, TX)])
        return carry

    lax.fori_loop(0, STEPS_DEV, own_forcing, 0, unroll=8)
    each(s == mid, sides[1].early, begin)

    yields = s == mid

    sides[0].goes, sides[1].goes = has_right, has_left & jnp.logical_not(yields)

    def pass_on(first, last):
        if first == 0:
            for copy in up_early:
                copy.wait_recv()
            for side in sides:
                each(side.goes, side.late, begin)
        for i in range(first, last):
            up_state[i].wait_recv()
            for side in sides:
                each(side.goes, [side.state[OWN + i]], begin)

    def next_own_forcing(n, carry):
        m = n + STEPS_DEV
        fill_forcing(forcing, 0, m, [(nc[m], kc2[pl.ds(n, 1)], 0, TX)])
        return carry

    @pl.when(asks)
    def _():
        pl.semaphore_wait(ready, 1)
        for copy in up_early + up_state:
            copy.start()

    @pl.when(core == 0)
    def _():
        pass_on(0, DEPTH)
        lax.fori_loop(0, 4, next_own_forcing, 0, unroll=4)

    def relay(side):
        for taken, given in zip(side.detour, side.relayed):
            each(side.is_relay, [taken], arrive)
            each(side.is_relay, [given], begin)

    relay(sides[0])

    for side in sides:
        for half in range(2):
            mine = slice(2 * half, 2 * half + 2)
            each(side.receives & (core == half), side.rates[mine], arrive)
            each(side.receives & (core == half), side.forward[mine], begin)
    for side in sides:
        for half in range(2):
            other = slice(2 - 2 * half, 4 - 2 * half)
            each(side.receives & (core == half), side.rates[other], arrive)

    x_of = lax.broadcasted_iota(jnp.int32, (TX, NY), 0)
    y_of = lax.broadcasted_iota(jnp.int32, (TX, NY), 1)
    first_half = x_of < 4
    is_first, is_end = x_of == 0, x_of == TX - 1

    def down_x(v):
        return pltpu.roll(v, 1, 0)

    def up_x(v):
        return pltpu.roll(v, TX - 1, 0)

    def make_rates(l, carry):
        def own(part):
            return part[0, l], part[1, l], part[2, l], part[3, l]

        dc, xc, yc, mc = own(rc)
        dl, xl, yl, ml = own(rl)
        dr, xr, yr, mr = own(rr)
        east_c, west_c = dc + jnp.maximum(-xc, 0.0), dc + jnp.maximum(xc, 0.0)
        east_l, west_l = dl + jnp.maximum(-xl, 0.0), dl + jnp.maximum(xl, 0.0)
        east_r, west_r = dr + jnp.maximum(-xr, 0.0), dr + jnp.maximum(xr, 0.0)
        dh = jnp.where(first_half, dr, dl)
        yh = jnp.where(first_half, yr, yl)
        mh = jnp.where(first_half, mr, ml)
        east_h = jnp.where(first_half, east_r, east_l)
        west_h = jnp.where(first_half, west_r, west_l)
        from_west = (
            jnp.where(is_first, down_x(east_l), down_x(east_c)),
            jnp.where(first_half, jnp.where(is_first, down_x(east_c), down_x(east_r)), down_x(east_l)),
        )
        from_east = (
            jnp.where(is_end, up_x(west_r), up_x(west_c)),
            jnp.where(first_half, up_x(west_r), jnp.where(is_end, up_x(west_c), up_x(west_l))),
        )
        for which, (d, e, w, y, m) in enumerate(
            ((dc, east_c, west_c, yc, mc), (dh, east_h, west_h, yh, mh))
        ):
            north, south = d + jnp.maximum(-y, 0.0), d + jnp.maximum(y, 0.0)
            coef[l, which, 0] = 1.0 - (e + w + north + south + m + m)
            coef[l, which, 1] = from_west[which]
            coef[l, which, 2] = from_east[which]
            coef[l, which, 3] = jnp.where(y_of == 0, 0.0, pltpu.roll(north, 1, 1))
            coef[l, which, 4] = jnp.where(y_of == NY - 1, 0.0, pltpu.roll(south, NY - 1, 1))
            coef[l, which, 5] = m
        return carry

    lax.fori_loop(0, LEV, make_rates, 0, unroll=2)

    @pl.when(core == 1)
    def _():
        pass_on(0, 2)
        lax.fori_loop(0, 4, next_own_forcing, 0, unroll=4)

    for side in sides:
        each(side.receives, side.early, arrive)

    def halo_forcing(n, carry):
        fill_forcing(forcing, 1, n, [(nl[n], kl[pl.ds(n, 1)], 4, TX), (nr[n], kr[pl.ds(n, 1)], 0, 4)])
        return carry

    lax.fori_loop(0, STEPS_DEV, halo_forcing, 0, unroll=8)

    @pl.when(core == 1)
    def _():
        pass_on(2, DEPTH)

    each(yields, sides[1].late + sides[1].state[OWN:], begin)

    @pl.when(s == 0)
    def _():
        pl.semaphore_wait(ready, 1)

    relay(sides[1])


    def next_forcing(n, carry):
        m = n + STEPS_DEV
        fill_forcing(forcing, 1, m, [(nl[m], kl2[pl.ds(n, 1)], 4, TX), (nr[m], kr2[pl.ds(n, 1)], 0, 4)])
        return carry

    def sweep(first, loads, dst, plane, last):
        def level(l):
            own_mix = coef[l, 0, 5]
            halo_mix = None if last else coef[l, 1, 5]
            found = []
            for load in loads:
                c, h = load(l)
                whole = h
                if isinstance(h, tuple):
                    whole = jnp.where(first_half, h[1], h[0])
                found.append((c, h, whole, (own_mix * c, None if last else halo_mix * whole)))
            return found

        levels = [level(0), level(1)]
        for l in range(LEV):
            if 0 < l < LEV - 1:
                levels.append(level(l + 1))
            factor = [[coef[l, which, k] for k in range(5)] for which in range(1 if last else 2)]
            for p in range(GROUP):
                c, h, whole, _ = levels[l][p]
                cd, cu = down_x(c), up_x(c)
                if isinstance(h, tuple):
                    ld, rd, lu, ru = down_x(h[0]), down_x(h[1]), up_x(h[0]), up_x(h[1])
                    hd, hu = jnp.where(first_half, rd, ld), jnp.where(first_half, ru, lu)
                else:
                    hd, hu = down_x(whole), up_x(whole)
                    ld, ru = hd, hu
                todo = [(c, jnp.where(is_first, ld, cd), jnp.where(is_end, ru, cu))]
                if not last:
                    todo.append((whole, jnp.where(is_first, cd, hd), jnp.where(is_end, cu, hu)))
                for which, (v, west, east) in enumerate(todo):
                    keep, from_west, from_east, from_south, from_north = factor[which]
                    total = forcing[plane + p, l, which] + keep * v
                    total = total + (from_west * west + from_east * east)
                    total = total + (
                        from_south * pltpu.roll(v, 1, 1) + from_north * pltpu.roll(v, NY - 1, 1)
                    )
                    for k in (l - 1, l + 1):
                        if 0 <= k < LEV:
                            total = total + levels[k][p][3][which]
                    if last:
                        out[first + p, l] = total
                    else:
                        dst[p, l, which] = total

    def chain(group, carry):
        first = group * GROUP
        for k in range(STEPS_DEV):
            for side in sides:
                each(side.receives & (group == k // GROUP), [side.state[k]], arrive)

        @pl.when(group == (OWN + 1) // GROUP)
        def _():
            for side in sides:
                each(side.receives, side.late, arrive)
            lax.fori_loop(0, 4, next_forcing, 0, unroll=4)

        def start(p):
            return lambda l: (ac[first + p, l], (hl[first + p, l], hr[first + p, l]))

        sweep(first, [start(p) for p in range(GROUP)], va, first + 4, False)

        @pl.when(is_last & (group == OWN // GROUP))
        def _():
            va[OWN % GROUP] = forcing[STEPS_DEV - 1]

        bufs = (va, vb)
        for k in range(2, DEPTH + 1):
            src, dst = bufs[k % 2], bufs[(k + 1) % 2]

            @pl.when(is_last & (group == (k + 2) // GROUP))
            def _(src=src, p=(k + 2) % GROUP):
                src[p, :, 0] = CIRC_ALPHA * (src[p, :, 0] - ac[OWN])
                outside = jnp.where(first_half[None], hr[OWN], hl[OWN])
                src[p, :, 1] = CIRC_ALPHA * (src[p, :, 1] - outside)

            def middle(p, src=src):
                return lambda l: (src[p, l, 0], src[p, l, 1])

            sweep(first, [middle(p) for p in range(GROUP)], dst, first + DEPTH - k, k == DEPTH)
        return carry

    lax.fori_loop(0, STEPS_DEV // GROUP, chain, 0)

    for side in sides:
        each(side.sends, side.early + side.late + side.state[OWN:], leave)
        each(side.sends, [side.state[i] for i in side.straight], leave)
        each(side.sends & jnp.logical_not(side.is_entry), [side.state[i] for i in side.far], leave)
        each(side.is_entry, side.detour, leave)
        each(side.is_relay, side.relayed, leave)
        for half in range(2):
            mine = slice(2 * half, 2 * half + 2)
            each(side.sends & (core == half), side.rates[mine], leave)
            each(side.receives & (core == half), side.forward[mine], leave)
    for copy in up_early + up_state:
        copy.wait_send()


def body(adjoint_iterate, innovations, station_cells, diffusivity, wind_x, wind_y, vertical_mixing):
    field = (LEV, TX, NY)
    f32, i32 = jnp.float32, jnp.int32
    scratch = (
        [pltpu.VMEM((STEPS_DEV,) + field, f32)] * 3
        + [pltpu.VMEM((STEPS_DEV + 4, LEV, NY), f32)] * 3
        + [pltpu.VMEM((STEPS_DEV, NY), i32)] * 6
        + [pltpu.VMEM((4,) + field, f32)] * 3
        + [pltpu.VMEM((LEV, 2, 6, TX, NY), f32)]
        + [pltpu.VMEM((STEPS_DEV + 4, LEV, 2, TX, NY), f32)]
        + [pltpu.VMEM((GROUP, LEV, 2, TX, NY), f32)] * 2
        + [pltpu.VMEM((OWN,) + field, f32)]
        + [pltpu.SemaphoreType.DMA((TRANSFERS,))] * 2
        + [pltpu.SemaphoreType.DMA((7,)), pltpu.SemaphoreType.REGULAR]
    )
    return pl.pallas_call(
        functools.partial(kernel, lax.axis_size("tm"), lax.axis_size("space")),
        out_shape=jax.ShapeDtypeStruct((STEPS_DEV,) + field, f32),
        in_specs=[pl.BlockSpec(memory_space=pl.ANY)] * 7,
        out_specs=pl.BlockSpec(memory_space=pltpu.VMEM),
        scratch_shapes=scratch,
        compiler_params=pltpu.CompilerParams(
            collective_id=0, has_side_effects=True, vmem_limit_bytes=24 * 2**20
        ),
        name="update",
    )(*[
        pltpu.with_memory_space_constraint(x, pltpu.HBM)
        for x in (adjoint_iterate, innovations, station_cells, diffusivity, wind_x, wind_y, vertical_mixing)
    ])


def solution(mesh):
    in_specs = (
        P("tm", None, "space", None),
        P("tm", None, "space"),
        P("tm", "space"),
        P(None, "space", None),
        P(None, "space", None),
        P(None, "space", None),
        P(None, "space", None),
    )
    out_specs = P("tm", None, "space", None)
    return jax.shard_map(body, mesh=mesh, in_specs=in_specs, out_specs=out_specs, check_vma=False)
```

```python
import functools

import jax
import jax.numpy as jnp
from jax import lax
from jax.experimental import pallas as pl
from jax.experimental.pallas import tpu as pltpu
from jax.sharding import PartitionSpec as P

MESH = pl.DeviceIdType.MESH

LEV = 16
TX = 8
NY = 128
STEPS_DEV = 8
DEPTH = 5
CIRC_ALPHA = 0.1
GROUP = 2

RATES, FORWARD, INNOV, CELLS, STATE, INNOV_UP, CELLS_UP, RELAY, PER_SIDE = 0, 4, 8, 9, 10, 18, 19, 20, 23
INNOV_T, CELLS_T, STATE_T = 2 * PER_SIDE, 2 * PER_SIDE + 1, 2 * PER_SIDE + 2
TRANSFERS = STATE_T + DEPTH
OWN = STEPS_DEV - DEPTH


def fill_forcing(forcing, which, plane, parts):
    x_of = lax.broadcasted_iota(jnp.int32, (TX, NY), 0)
    y_of = lax.broadcasted_iota(jnp.int32, (NY, NY), 0)
    total = None
    for values, cells, low, high in parts:
        column = cells // NY
        row = cells % NY
        mask = (column == x_of) & (x_of >= low) & (x_of < high)
        head = values.astype(jnp.bfloat16).astype(jnp.float32)
        rest = values - head
        pieces = [
            jnp.where(mask[None], piece[:, None, :], 0.0).reshape(LEV * TX, NY).astype(jnp.bfloat16)
            for piece in (head, rest)
        ]
        hot = jnp.where(row == y_of, 1.0, 0.0).astype(jnp.bfloat16)
        part = lax.dot_general(
            jnp.concatenate(pieces, axis=1),
            jnp.concatenate([hot, hot], axis=1),
            (((1,), (1,)), ((), ())),
            preferred_element_type=jnp.float32,
        )
        total = part if total is None else total + part
    forcing[plane, :, which] = total.reshape(LEV, TX, NY)


def kernel(
    time_parts, tiles,
    a, innov, cells, dif, wx, wy, vm, out,
    ac, hl, hr, nc, nl, nr, kc, kl, kr, kc2, kl2, kr2, rc, rl, rr, coef, forcing, va, vb, hold,
    send, recv, local, ready,
):
    t = lax.axis_index("tm")
    s = lax.axis_index("space")
    before = lax.rem(t + time_parts - 1, time_parts)
    after = lax.rem(t + 1, time_parts)
    core = lax.rem(t, 2)
    sibling = t + 1 - 2 * core
    mid = tiles // 2
    has_left = s > 0
    has_right = s < tiles - 1
    is_last = t == time_parts - 1
    asks, says = (core == 0) & (s == mid - 1), (core == 1) & (s == mid - 1)

    barrier = pltpu.get_barrier_semaphore()

    def greet(device):
        pl.semaphore_signal(barrier, inc=1, device_id=device, device_id_type=MESH)

    greet((sibling, s))

    @pl.when(jnp.logical_not(says))
    def _():
        greet((after, s))

    @pl.when(asks)
    def _():
        greet((before, s))

    for here, device in (
        (has_left, s - 1),
        (has_right, s + 1),
        (s == 0, mid - 1),
        (s == 0, mid),
        (s == tiles - 1, mid - 1),
        (s == mid, tiles - 1),
    ):

        @pl.when(here)
        def _(device=device):
            greet((t, device))

    fields = (dif, wx, wy, vm)
    loads = [
        pltpu.make_async_copy(innov, nc.at[pl.ds(0, STEPS_DEV)], local.at[0]),
        pltpu.make_async_copy(cells, kc, local.at[1]),
        pltpu.make_async_copy(a.at[pl.ds(DEPTH, OWN)], ac.at[pl.ds(0, OWN)], local.at[2]),
    ] + [pltpu.make_async_copy(f, rc.at[i], local.at[3 + i]) for i, f in enumerate(fields)]
    for load in loads:
        load.start()

    def remote(number, src, dst, device, landing=None):
        return pltpu.make_async_remote_copy(
            src_ref=src, dst_ref=dst, send_sem=send.at[number],
            recv_sem=recv.at[number if landing is None else landing],
            device_id=device, device_id_type=MESH,
        )

    class Side:
        def __init__(self, base, step, first, halo, inn, cel, cel_up, rat, relay, entry, far):
            self.sends, self.receives = (has_right, has_left) if step > 0 else (has_left, has_right)
            self.zeros = (halo, inn, cel, cel_up, rat)
            to = (t, s + step)
            cols = pl.ds(first, 5)
            edge = pl.ds(4, 4) if step > 0 else pl.ds(0, 4)
            cut = [cols if i < 2 else edge for i in range(4)]
            self.rates = [
                remote(base + RATES + i, f.at[:, cut[i]], rat.at[i, :, cut[i]], to)
                for i, f in enumerate(fields)
            ]
            self.forward = [
                remote(base + FORWARD + i, rat.at[i, :, cut[i]], rat.at[i, :, cut[i]], (sibling, s), base + RATES + i)
                for i in range(4)
            ]
            self.early = [
                remote(base + CELLS, cells, cel, to),
                remote(base + INNOV, innov, inn.at[pl.ds(0, STEPS_DEV)], to),
            ]
            self.late = [
                remote(base + CELLS_UP, kc2, cel_up, to),
                remote(base + INNOV_UP, nc.at[pl.ds(STEPS_DEV, 4)], inn.at[pl.ds(STEPS_DEV, 4)], to),
            ]
            self.is_relay, self.is_entry = s == relay, s == entry
            self.state = [
                remote(base + STATE + i, a.at[i + DEPTH, :, cols], halo.at[i, :, cols], to)
                for i in range(OWN)
            ] + [
                remote(base + STATE + i, ac.at[i, :, cols], halo.at[i, :, cols], to)
                for i in range(OWN, STEPS_DEV)
            ]
            self.straight, self.far = [i for i in range(OWN) if i not in far], far
            self.detour = [
                remote(base + STATE + i, a.at[i + DEPTH, :, cols], hold.at[i, :, cols], (t, relay), base + RELAY + i)
                for i in far
            ]
            self.relayed = [
                remote(base + RELAY + i, hold.at[i, :, cols], halo.at[i, :, cols], (t, entry + step), base + STATE + i)
                for i in far
            ]

    sides = (
        Side(0, 1, 3, hl, nl, kl, kl2, rl, tiles - 1, mid - 1, (0, 1, 2)),
        Side(PER_SIDE, -1, 0, hr, nr, kr, kr2, rr, 0, mid, (0, 1, 2)),
    )
    up_early = [
        remote(CELLS_T, cells, kc2, (before, s)),
        remote(INNOV_T, innov.at[pl.ds(0, 4)], nc.at[pl.ds(STEPS_DEV, 4)], (before, s)),
    ]
    up_state = [remote(STATE_T + i, a.at[i], ac.at[OWN + i], (before, s)) for i in range(DEPTH)]

    for side in sides:

        @pl.when(jnp.logical_not(side.receives))
        def _(side=side):
            for ref in side.zeros:
                ref[...] = jnp.zeros(ref.shape, ref.dtype)

    def each(condition, copies, act):
        @pl.when(condition)
        def _():
            for copy in copies:
                act(copy)

    def begin(copy):
        copy.start()

    def arrive(copy):
        copy.wait_recv()

    def leave(copy):
        copy.wait_send()

    def number(flag):
        return flag.astype(jnp.int32)

    pl.semaphore_wait(
        barrier,
        2 + number(has_left) + number(has_right) + 2 * number(s == mid - 1) + number(s == mid)
        + number(s == tiles - 1) + number(says) - number(asks),
    )

    @pl.when(s == mid - 1)
    def _():
        pl.semaphore_signal(ready, inc=1, device_id=(t, 0), device_id_type=MESH)

    @pl.when(says)
    def _():
        pl.semaphore_signal(ready, inc=1, device_id=(after, s), device_id_type=MESH)

    each(jnp.logical_not(asks), up_early + up_state, begin)
    for side in sides:
        for half in range(2):
            each(side.sends & (core == half), side.rates[2 * half : 2 * half + 2], begin)
    for side in sides:
        each(side.sends if side is sides[0] else side.sends & (s != mid), side.early, begin)
        each(side.is_entry, side.detour, begin)

    for load in loads:
        load.wait()
    for i in range(OWN):
        for side in sides:
            near = side.sends if i in side.straight else side.sends & jnp.logical_not(side.is_entry)
            each(near, [side.state[i]], begin)

    def own_forcing(n, carry):
        fill_forcing(forcing, 0, n, [(nc[n], kc[pl.ds(n, 1)], 0, TX)])
        return carry

    lax.fori_loop(0, STEPS_DEV, own_forcing, 0, unroll=8)
    each(s == mid, sides[1].early, begin)

    yields = s == mid

    sides[0].goes, sides[1].goes = has_right, has_left & jnp.logical_not(yields)

    def pass_on(first, last):
        if first == 0:
            for copy in up_early:
                copy.wait_recv()
            for side in sides:
                each(side.goes, side.late, begin)
        for i in range(first, last):
            up_state[i].wait_recv()
            for side in sides:
                each(side.goes, [side.state[OWN + i]], begin)

    def next_own_forcing(n, carry):
        m = n + STEPS_DEV
        fill_forcing(forcing, 0, m, [(nc[m], kc2[pl.ds(n, 1)], 0, TX)])
        return carry

    @pl.when(asks)
    def _():
        pl.semaphore_wait(ready, 1)
        for copy in up_early + up_state:
            copy.start()

    @pl.when(core == 0)
    def _():
        pass_on(0, DEPTH)
        lax.fori_loop(0, 4, next_own_forcing, 0, unroll=4)

    def relay(side):
        for taken, given in zip(side.detour, side.relayed):
            each(side.is_relay, [taken], arrive)
            each(side.is_relay, [given], begin)

    relay(sides[0])

    for side in sides:
        for half in range(2):
            mine = slice(2 * half, 2 * half + 2)
            each(side.receives & (core == half), side.rates[mine], arrive)
            each(side.receives & (core == half), side.forward[mine], begin)
    for side in sides:
        for half in range(2):
            other = slice(2 - 2 * half, 4 - 2 * half)
            each(side.receives & (core == half), side.rates[other], arrive)

    x_of = lax.broadcasted_iota(jnp.int32, (TX, NY), 0)
    y_of = lax.broadcasted_iota(jnp.int32, (TX, NY), 1)
    first_half = x_of < 4
    is_first, is_end = x_of == 0, x_of == TX - 1

    def down_x(v):
        return pltpu.roll(v, 1, 0)

    def up_x(v):
        return pltpu.roll(v, TX - 1, 0)

    def make_rates(l, carry):
        def own(part):
            return part[0, l], part[1, l], part[2, l], part[3, l]

        dc, xc, yc, mc = own(rc)
        dl, xl, yl, ml = own(rl)
        dr, xr, yr, mr = own(rr)
        east_c, west_c = dc + jnp.maximum(-xc, 0.0), dc + jnp.maximum(xc, 0.0)
        east_l, west_l = dl + jnp.maximum(-xl, 0.0), dl + jnp.maximum(xl, 0.0)
        east_r, west_r = dr + jnp.maximum(-xr, 0.0), dr + jnp.maximum(xr, 0.0)
        dh = jnp.where(first_half, dr, dl)
        yh = jnp.where(first_half, yr, yl)
        mh = jnp.where(first_half, mr, ml)
        east_h = jnp.where(first_half, east_r, east_l)
        west_h = jnp.where(first_half, west_r, west_l)
        from_west = (
            jnp.where(is_first, down_x(east_l), down_x(east_c)),
            jnp.where(first_half, jnp.where(is_first, down_x(east_c), down_x(east_r)), down_x(east_l)),
        )
        from_east = (
            jnp.where(is_end, up_x(west_r), up_x(west_c)),
            jnp.where(first_half, up_x(west_r), jnp.where(is_end, up_x(west_c), up_x(west_l))),
        )
        for which, (d, e, w, y, m) in enumerate(
            ((dc, east_c, west_c, yc, mc), (dh, east_h, west_h, yh, mh))
        ):
            north, south = d + jnp.maximum(-y, 0.0), d + jnp.maximum(y, 0.0)
            coef[l, which, 0] = 1.0 - (e + w + north + south + m + m)
            coef[l, which, 1] = from_west[which]
            coef[l, which, 2] = from_east[which]
            coef[l, which, 3] = jnp.where(y_of == 0, 0.0, pltpu.roll(north, 1, 1))
            coef[l, which, 4] = jnp.where(y_of == NY - 1, 0.0, pltpu.roll(south, NY - 1, 1))
            coef[l, which, 5] = m
        return carry

    lax.fori_loop(0, LEV, make_rates, 0, unroll=2)

    @pl.when(core == 1)
    def _():
        pass_on(0, 4)
        lax.fori_loop(0, 4, next_own_forcing, 0, unroll=4)

    for side in sides:
        each(side.receives, side.early, arrive)

    def halo_forcing(n, carry):
        fill_forcing(forcing, 1, n, [(nl[n], kl[pl.ds(n, 1)], 4, TX), (nr[n], kr[pl.ds(n, 1)], 0, 4)])
        return carry

    lax.fori_loop(0, STEPS_DEV, halo_forcing, 0, unroll=8)

    @pl.when(core == 1)
    def _():
        pass_on(4, DEPTH)

    each(yields, sides[1].late + sides[1].state[OWN:], begin)

    @pl.when(s == 0)
    def _():
        pl.semaphore_wait(ready, 1)

    relay(sides[1])


    def next_forcing(n, carry):
        m = n + STEPS_DEV
        fill_forcing(forcing, 1, m, [(nl[m], kl2[pl.ds(n, 1)], 4, TX), (nr[m], kr2[pl.ds(n, 1)], 0, 4)])
        return carry

    def sweep(first, loads, dst, plane, last):
        def level(l):
            own_mix = coef[l, 0, 5]
            halo_mix = None if last else coef[l, 1, 5]
            found = []
            for load in loads:
                c, h = load(l)
                whole = h
                if isinstance(h, tuple):
                    whole = jnp.where(first_half, h[1], h[0])
                found.append((c, h, whole, (own_mix * c, None if last else halo_mix * whole)))
            return found

        levels = [level(0), level(1)]
        for l in range(LEV):
            if 0 < l < LEV - 1:
                levels.append(level(l + 1))
            factor = [[coef[l, which, k] for k in range(5)] for which in range(1 if last else 2)]
            for p in range(GROUP):
                c, h, whole, _ = levels[l][p]
                cd, cu = down_x(c), up_x(c)
                if isinstance(h, tuple):
                    ld, rd, lu, ru = down_x(h[0]), down_x(h[1]), up_x(h[0]), up_x(h[1])
                    hd, hu = jnp.where(first_half, rd, ld), jnp.where(first_half, ru, lu)
                else:
                    hd, hu = down_x(whole), up_x(whole)
                    ld, ru = hd, hu
                todo = [(c, jnp.where(is_first, ld, cd), jnp.where(is_end, ru, cu))]
                if not last:
                    todo.append((whole, jnp.where(is_first, cd, hd), jnp.where(is_end, cu, hu)))
                for which, (v, west, east) in enumerate(todo):
                    keep, from_west, from_east, from_south, from_north = factor[which]
                    total = forcing[plane + p, l, which] + keep * v
                    total = total + (from_west * west + from_east * east)
                    total = total + (
                        from_south * pltpu.roll(v, 1, 1) + from_north * pltpu.roll(v, NY - 1, 1)
                    )
                    for k in (l - 1, l + 1):
                        if 0 <= k < LEV:
                            total = total + levels[k][p][3][which]
                    if last:
                        out[first + p, l] = total
                    else:
                        dst[p, l, which] = total

    def chain(group, carry):
        first = group * GROUP

        @pl.when(group == OWN // GROUP)
        def _():
            for side in sides:
                each(side.receives, side.late, arrive)
            lax.fori_loop(0, 4, next_forcing, 0, unroll=4)

        for k in range(STEPS_DEV):
            for side in sides:
                each(side.receives & (group == k // GROUP), [side.state[k]], arrive)

        def start(p):
            return lambda l: (ac[first + p, l], (hl[first + p, l], hr[first + p, l]))

        sweep(first, [start(p) for p in range(GROUP)], va, first + 4, False)

        @pl.when(is_last & (group == OWN // GROUP))
        def _():
            va[OWN % GROUP] = forcing[STEPS_DEV - 1]

        bufs = (va, vb)
        for k in range(2, DEPTH + 1):
            src, dst = bufs[k % 2], bufs[(k + 1) % 2]

            @pl.when(is_last & (group == (k + 2) // GROUP))
            def _(src=src, p=(k + 2) % GROUP):
                src[p, :, 0] = CIRC_ALPHA * (src[p, :, 0] - ac[OWN])
                outside = jnp.where(first_half[None], hr[OWN], hl[OWN])
                src[p, :, 1] = CIRC_ALPHA * (src[p, :, 1] - outside)

            def middle(p, src=src):
                return lambda l: (src[p, l, 0], src[p, l, 1])

            sweep(first, [middle(p) for p in range(GROUP)], dst, first + DEPTH - k, k == DEPTH)
        return carry

    lax.fori_loop(0, STEPS_DEV // GROUP, chain, 0)

    for side in sides:
        each(side.sends, side.early + side.late + side.state[OWN:], leave)
        each(side.sends, [side.state[i] for i in side.straight], leave)
        each(side.sends & jnp.logical_not(side.is_entry), [side.state[i] for i in side.far], leave)
        each(side.is_entry, side.detour, leave)
        each(side.is_relay, side.relayed, leave)
        for half in range(2):
            mine = slice(2 * half, 2 * half + 2)
            each(side.sends & (core == half), side.rates[mine], leave)
            each(side.receives & (core == half), side.forward[mine], leave)
    for copy in up_early + up_state:
        copy.wait_send()


def body(adjoint_iterate, innovations, station_cells, diffusivity, wind_x, wind_y, vertical_mixing):
    field = (LEV, TX, NY)
    f32, i32 = jnp.float32, jnp.int32
    scratch = (
        [pltpu.VMEM((STEPS_DEV,) + field, f32)] * 3
        + [pltpu.VMEM((STEPS_DEV + 4, LEV, NY), f32)] * 3
        + [pltpu.VMEM((STEPS_DEV, NY), i32)] * 6
        + [pltpu.VMEM((4,) + field, f32)] * 3
        + [pltpu.VMEM((LEV, 2, 6, TX, NY), f32)]
        + [pltpu.VMEM((STEPS_DEV + 4, LEV, 2, TX, NY), f32)]
        + [pltpu.VMEM((GROUP, LEV, 2, TX, NY), f32)] * 2
        + [pltpu.VMEM((OWN,) + field, f32)]
        + [pltpu.SemaphoreType.DMA((TRANSFERS,))] * 2
        + [pltpu.SemaphoreType.DMA((7,)), pltpu.SemaphoreType.REGULAR]
    )
    return pl.pallas_call(
        functools.partial(kernel, lax.axis_size("tm"), lax.axis_size("space")),
        out_shape=jax.ShapeDtypeStruct((STEPS_DEV,) + field, f32),
        in_specs=[pl.BlockSpec(memory_space=pl.ANY)] * 7,
        out_specs=pl.BlockSpec(memory_space=pltpu.VMEM),
        scratch_shapes=scratch,
        compiler_params=pltpu.CompilerParams(
            collective_id=0, has_side_effects=True, vmem_limit_bytes=24 * 2**20
        ),
        name="update",
    )(*[
        pltpu.with_memory_space_constraint(x, pltpu.HBM)
        for x in (adjoint_iterate, innovations, station_cells, diffusivity, wind_x, wind_y, vertical_mixing)
    ])


def solution(mesh):
    in_specs = (
        P("tm", None, "space", None),
        P("tm", None, "space"),
        P("tm", "space"),
        P(None, "space", None),
        P(None, "space", None),
        P(None, "space", None),
        P(None, "space", None),
    )
    out_specs = P("tm", None, "space", None)
    return jax.shard_map(body, mesh=mesh, in_specs=in_specs, out_specs=out_specs, check_vma=False)
```

```python
import functools

import jax
import jax.numpy as jnp
from jax import lax
from jax.experimental import pallas as pl
from jax.experimental.pallas import tpu as pltpu
from jax.sharding import PartitionSpec as P

MESH = pl.DeviceIdType.MESH

LEV = 16
TX = 8
NY = 128
STEPS_DEV = 8
DEPTH = 5
CIRC_ALPHA = 0.1
GROUP = 2

RATES, FORWARD, INNOV, CELLS, STATE, INNOV_UP, CELLS_UP, RELAY, PER_SIDE = 0, 4, 8, 9, 10, 18, 19, 20, 23
INNOV_T, CELLS_T, STATE_T = 2 * PER_SIDE, 2 * PER_SIDE + 1, 2 * PER_SIDE + 2
TRANSFERS = STATE_T + DEPTH
OWN = STEPS_DEV - DEPTH


def fill_forcing(forcing, which, plane, parts):
    x_of = lax.broadcasted_iota(jnp.int32, (TX, NY), 0)
    y_of = lax.broadcasted_iota(jnp.int32, (NY, NY), 0)
    total = None
    for values, cells, low, high in parts:
        column = cells // NY
        row = cells % NY
        mask = (column == x_of) & (x_of >= low) & (x_of < high)
        head = values.astype(jnp.bfloat16).astype(jnp.float32)
        rest = values - head
        pieces = [
            jnp.where(mask[None], piece[:, None, :], 0.0).reshape(LEV * TX, NY).astype(jnp.bfloat16)
            for piece in (head, rest)
        ]
        hot = jnp.where(row == y_of, 1.0, 0.0).astype(jnp.bfloat16)
        part = lax.dot_general(
            jnp.concatenate(pieces, axis=1),
            jnp.concatenate([hot, hot], axis=1),
            (((1,), (1,)), ((), ())),
            preferred_element_type=jnp.float32,
        )
        total = part if total is None else total + part
    forcing[plane, :, which] = total.reshape(LEV, TX, NY)


def kernel(
    time_parts, tiles,
    a, innov, cells, dif, wx, wy, vm, out,
    ac, hl, hr, nc, nl, nr, kc, kl, kr, kc2, kl2, kr2, rc, rl, rr, coef, forcing, va, vb, hold,
    send, recv, local, ready,
):
    t = lax.axis_index("tm")
    s = lax.axis_index("space")
    before = lax.rem(t + time_parts - 1, time_parts)
    after = lax.rem(t + 1, time_parts)
    core = lax.rem(t, 2)
    sibling = t + 1 - 2 * core
    mid = tiles // 2
    has_left = s > 0
    has_right = s < tiles - 1
    is_last = t == time_parts - 1
    asks, says = (core == 0) & (s == mid - 1), (core == 1) & (s == mid - 1)

    barrier = pltpu.get_barrier_semaphore()

    def greet(device):
        pl.semaphore_signal(barrier, inc=1, device_id=device, device_id_type=MESH)

    greet((sibling, s))

    @pl.when(jnp.logical_not(says))
    def _():
        greet((after, s))

    @pl.when(asks)
    def _():
        greet((before, s))

    for here, device in (
        (has_left, s - 1),
        (has_right, s + 1),
        (s == 0, mid - 1),
        (s == 0, mid),
        (s == tiles - 1, mid - 1),
        (s == mid, tiles - 1),
    ):

        @pl.when(here)
        def _(device=device):
            greet((t, device))

    fields = (dif, wx, wy, vm)
    loads = [
        pltpu.make_async_copy(innov, nc.at[pl.ds(0, STEPS_DEV)], local.at[0]),
        pltpu.make_async_copy(cells, kc, local.at[1]),
        pltpu.make_async_copy(a.at[pl.ds(DEPTH, OWN)], ac.at[pl.ds(0, OWN)], local.at[2]),
    ] + [pltpu.make_async_copy(f, rc.at[i], local.at[3 + i]) for i, f in enumerate(fields)]
    for load in loads:
        load.start()

    def remote(number, src, dst, device, landing=None):
        return pltpu.make_async_remote_copy(
            src_ref=src, dst_ref=dst, send_sem=send.at[number],
            recv_sem=recv.at[number if landing is None else landing],
            device_id=device, device_id_type=MESH,
        )

    class Side:
        def __init__(self, base, step, first, halo, inn, cel, cel_up, rat, relay, entry, far):
            self.sends, self.receives = (has_right, has_left) if step > 0 else (has_left, has_right)
            self.zeros = (halo, inn, cel, cel_up, rat)
            to = (t, s + step)
            cols = pl.ds(first, 5)
            edge = pl.ds(4, 4) if step > 0 else pl.ds(0, 4)
            cut = [cols if i < 2 else edge for i in range(4)]
            self.rates = [
                remote(base + RATES + i, f.at[:, cut[i]], rat.at[i, :, cut[i]], to)
                for i, f in enumerate(fields)
            ]
            self.forward = [
                remote(base + FORWARD + i, rat.at[i, :, cut[i]], rat.at[i, :, cut[i]], (sibling, s), base + RATES + i)
                for i in range(4)
            ]
            self.early = [
                remote(base + CELLS, cells, cel, to),
                remote(base + INNOV, innov, inn.at[pl.ds(0, STEPS_DEV)], to),
            ]
            self.late = [
                remote(base + CELLS_UP, kc2, cel_up, to),
                remote(base + INNOV_UP, nc.at[pl.ds(STEPS_DEV, 4)], inn.at[pl.ds(STEPS_DEV, 4)], to),
            ]
            self.is_relay, self.is_entry = s == relay, s == entry
            self.state = [
                remote(base + STATE + i, a.at[i + DEPTH, :, cols], halo.at[i, :, cols], to)
                for i in range(OWN)
            ] + [
                remote(base + STATE + i, ac.at[i, :, cols], halo.at[i, :, cols], to)
                for i in range(OWN, STEPS_DEV)
            ]
            self.straight, self.far = [i for i in range(OWN) if i not in far], far
            self.detour = [
                remote(base + STATE + i, a.at[i + DEPTH, :, cols], hold.at[i, :, cols], (t, relay), base + RELAY + i)
                for i in far
            ]
            self.relayed = [
                remote(base + RELAY + i, hold.at[i, :, cols], halo.at[i, :, cols], (t, entry + step), base + STATE + i)
                for i in far
            ]

    sides = (
        Side(0, 1, 3, hl, nl, kl, kl2, rl, tiles - 1, mid - 1, (0, 1, 2)),
        Side(PER_SIDE, -1, 0, hr, nr, kr, kr2, rr, 0, mid, (0, 1, 2)),
    )
    up_early = [
        remote(CELLS_T, cells, kc2, (before, s)),
        remote(INNOV_T, innov.at[pl.ds(0, 4)], nc.at[pl.ds(STEPS_DEV, 4)], (before, s)),
    ]
    up_state = [remote(STATE_T + i, a.at[i], ac.at[OWN + i], (before, s)) for i in range(DEPTH)]

    for side in sides:

        @pl.when(jnp.logical_not(side.receives))
        def _(side=side):
            for ref in side.zeros:
                ref[...] = jnp.zeros(ref.shape, ref.dtype)

    def each(condition, copies, act):
        @pl.when(condition)
        def _():
            for copy in copies:
                act(copy)

    def begin(copy):
        copy.start()

    def arrive(copy):
        copy.wait_recv()

    def leave(copy):
        copy.wait_send()

    def number(flag):
        return flag.astype(jnp.int32)

    pl.semaphore_wait(
        barrier,
        2 + number(has_left) + number(has_right) + 2 * number(s == mid - 1) + number(s == mid)
        + number(s == tiles - 1) + number(says) - number(asks),
    )

    @pl.when(s == mid - 1)
    def _():
        pl.semaphore_signal(ready, inc=1, device_id=(t, 0), device_id_type=MESH)

    @pl.when(says)
    def _():
        pl.semaphore_signal(ready, inc=1, device_id=(after, s), device_id_type=MESH)

    each(jnp.logical_not(asks), up_early + up_state, begin)
    for side in sides:
        for half in range(2):
            each(side.sends & (core == half), side.rates[2 * half : 2 * half + 2], begin)
    for side in sides:
        each(side.sends if side is sides[0] else side.sends & (s != mid), side.early, begin)
        each(side.is_entry, side.detour, begin)

    for load in loads:
        load.wait()
    for i in range(OWN):
        for side in sides:
            near = side.sends if i in side.straight else side.sends & jnp.logical_not(side.is_entry)
            each(near, [side.state[i]], begin)

    def own_forcing(n, carry):
        fill_forcing(forcing, 0, n, [(nc[n], kc[pl.ds(n, 1)], 0, TX)])
        return carry

    lax.fori_loop(0, STEPS_DEV, own_forcing, 0, unroll=8)
    each(s == mid, sides[1].early, begin)

    yields = s == mid

    sides[0].goes, sides[1].goes = has_right, has_left & jnp.logical_not(yields)

    def pass_on(first, last):
        if first == 0:
            for copy in up_early:
                copy.wait_recv()
            for side in sides:
                each(side.goes, side.late, begin)
        for i in range(first, last):
            up_state[i].wait_recv()
            for side in sides:
                each(side.goes, [side.state[OWN + i]], begin)

    def next_own_forcing(n, carry):
        m = n + STEPS_DEV
        fill_forcing(forcing, 0, m, [(nc[m], kc2[pl.ds(n, 1)], 0, TX)])
        return carry

    @pl.when(core == 0)
    def _():
        pass_on(0, DEPTH)
        lax.fori_loop(0, 4, next_own_forcing, 0, unroll=4)

    @pl.when(asks)
    def _():
        pl.semaphore_wait(ready, 1)
        for copy in up_early + up_state:
            copy.start()

    def relay(side):
        for taken, given in zip(side.detour, side.relayed):
            each(side.is_relay, [taken], arrive)
            each(side.is_relay, [given], begin)

    relay(sides[0])

    for side in sides:
        for half in range(2):
            mine = slice(2 * half, 2 * half + 2)
            each(side.receives & (core == half), side.rates[mine], arrive)
            each(side.receives & (core == half), side.forward[mine], begin)
    for side in sides:
        for half in range(2):
            other = slice(2 - 2 * half, 4 - 2 * half)
            each(side.receives & (core == half), side.rates[other], arrive)

    x_of = lax.broadcasted_iota(jnp.int32, (TX, NY), 0)
    y_of = lax.broadcasted_iota(jnp.int32, (TX, NY), 1)
    first_half = x_of < 4
    is_first, is_end = x_of == 0, x_of == TX - 1

    def down_x(v):
        return pltpu.roll(v, 1, 0)

    def up_x(v):
        return pltpu.roll(v, TX - 1, 0)

    def make_rates(l, carry):
        def own(part):
            return part[0, l], part[1, l], part[2, l], part[3, l]

        dc, xc, yc, mc = own(rc)
        dl, xl, yl, ml = own(rl)
        dr, xr, yr, mr = own(rr)
        east_c, west_c = dc + jnp.maximum(-xc, 0.0), dc + jnp.maximum(xc, 0.0)
        east_l, west_l = dl + jnp.maximum(-xl, 0.0), dl + jnp.maximum(xl, 0.0)
        east_r, west_r = dr + jnp.maximum(-xr, 0.0), dr + jnp.maximum(xr, 0.0)
        dh = jnp.where(first_half, dr, dl)
        yh = jnp.where(first_half, yr, yl)
        mh = jnp.where(first_half, mr, ml)
        east_h = jnp.where(first_half, east_r, east_l)
        west_h = jnp.where(first_half, west_r, west_l)
        from_west = (
            jnp.where(is_first, down_x(east_l), down_x(east_c)),
            jnp.where(first_half, jnp.where(is_first, down_x(east_c), down_x(east_r)), down_x(east_l)),
        )
        from_east = (
            jnp.where(is_end, up_x(west_r), up_x(west_c)),
            jnp.where(first_half, up_x(west_r), jnp.where(is_end, up_x(west_c), up_x(west_l))),
        )
        for which, (d, e, w, y, m) in enumerate(
            ((dc, east_c, west_c, yc, mc), (dh, east_h, west_h, yh, mh))
        ):
            north, south = d + jnp.maximum(-y, 0.0), d + jnp.maximum(y, 0.0)
            coef[l, which, 0] = 1.0 - (e + w + north + south + m + m)
            coef[l, which, 1] = from_west[which]
            coef[l, which, 2] = from_east[which]
            coef[l, which, 3] = jnp.where(y_of == 0, 0.0, pltpu.roll(north, 1, 1))
            coef[l, which, 4] = jnp.where(y_of == NY - 1, 0.0, pltpu.roll(south, NY - 1, 1))
            coef[l, which, 5] = m
        return carry

    lax.fori_loop(0, LEV, make_rates, 0, unroll=2)

    @pl.when(core == 1)
    def _():
        pass_on(0, 4)
        lax.fori_loop(0, 4, next_own_forcing, 0, unroll=4)

    for side in sides:
        each(side.receives, side.early, arrive)

    def halo_forcing(n, carry):
        fill_forcing(forcing, 1, n, [(nl[n], kl[pl.ds(n, 1)], 4, TX), (nr[n], kr[pl.ds(n, 1)], 0, 4)])
        return carry

    lax.fori_loop(0, STEPS_DEV, halo_forcing, 0, unroll=8)

    @pl.when(core == 1)
    def _():
        pass_on(4, DEPTH)

    each(yields, sides[1].late + sides[1].state[OWN:], begin)

    @pl.when(s == 0)
    def _():
        pl.semaphore_wait(ready, 1)

    relay(sides[1])


    def next_forcing(n, carry):
        m = n + STEPS_DEV
        fill_forcing(forcing, 1, m, [(nl[m], kl2[pl.ds(n, 1)], 4, TX), (nr[m], kr2[pl.ds(n, 1)], 0, 4)])
        return carry

    def sweep(first, loads, dst, plane, last):
        def level(l):
            own_mix = coef[l, 0, 5]
            halo_mix = None if last else coef[l, 1, 5]
            found = []
            for load in loads:
                c, h = load(l)
                whole = h
                if isinstance(h, tuple):
                    whole = jnp.where(first_half, h[1], h[0])
                found.append((c, h, whole, (own_mix * c, None if last else halo_mix * whole)))
            return found

        levels = [level(0), level(1)]
        for l in range(LEV):
            if 0 < l < LEV - 1:
                levels.append(level(l + 1))
            factor = [[coef[l, which, k] for k in range(5)] for which in range(1 if last else 2)]
            for p in range(GROUP):
                c, h, whole, _ = levels[l][p]
                cd, cu = down_x(c), up_x(c)
                if isinstance(h, tuple):
                    ld, rd, lu, ru = down_x(h[0]), down_x(h[1]), up_x(h[0]), up_x(h[1])
                    hd, hu = jnp.where(first_half, rd, ld), jnp.where(first_half, ru, lu)
                else:
                    hd, hu = down_x(whole), up_x(whole)
                    ld, ru = hd, hu
                todo = [(c, jnp.where(is_first, ld, cd), jnp.where(is_end, ru, cu))]
                if not last:
                    todo.append((whole, jnp.where(is_first, cd, hd), jnp.where(is_end, cu, hu)))
                for which, (v, west, east) in enumerate(todo):
                    keep, from_west, from_east, from_south, from_north = factor[which]
                    total = forcing[plane + p, l, which] + keep * v
                    total = total + (from_west * west + from_east * east)
                    total = total + (
                        from_south * pltpu.roll(v, 1, 1) + from_north * pltpu.roll(v, NY - 1, 1)
                    )
                    for k in (l - 1, l + 1):
                        if 0 <= k < LEV:
                            total = total + levels[k][p][3][which]
                    if last:
                        out[first + p, l] = total
                    else:
                        dst[p, l, which] = total

    def chain(group, carry):
        first = group * GROUP

        @pl.when(group == OWN // GROUP)
        def _():
            for side in sides:
                each(side.receives, side.late, arrive)
            lax.fori_loop(0, 4, next_forcing, 0, unroll=4)

        for k in range(STEPS_DEV):
            for side in sides:
                each(side.receives & (group == k // GROUP), [side.state[k]], arrive)

        def start(p):
            return lambda l: (ac[first + p, l], (hl[first + p, l], hr[first + p, l]))

        sweep(first, [start(p) for p in range(GROUP)], va, first + 4, False)

        @pl.when(is_last & (group == OWN // GROUP))
        def _():
            va[OWN % GROUP] = forcing[STEPS_DEV - 1]

        bufs = (va, vb)
        for k in range(2, DEPTH + 1):
            src, dst = bufs[k % 2], bufs[(k + 1) % 2]

            @pl.when(is_last & (group == (k + 2) // GROUP))
            def _(src=src, p=(k + 2) % GROUP):
                src[p, :, 0] = CIRC_ALPHA * (src[p, :, 0] - ac[OWN])
                outside = jnp.where(first_half[None], hr[OWN], hl[OWN])
                src[p, :, 1] = CIRC_ALPHA * (src[p, :, 1] - outside)

            def middle(p, src=src):
                return lambda l: (src[p, l, 0], src[p, l, 1])

            sweep(first, [middle(p) for p in range(GROUP)], dst, first + DEPTH - k, k == DEPTH)
        return carry

    lax.fori_loop(0, STEPS_DEV // GROUP, chain, 0)

    for side in sides:
        each(side.sends, side.early + side.late + side.state[OWN:], leave)
        each(side.sends, [side.state[i] for i in side.straight], leave)
        each(side.sends & jnp.logical_not(side.is_entry), [side.state[i] for i in side.far], leave)
        each(side.is_entry, side.detour, leave)
        each(side.is_relay, side.relayed, leave)
        for half in range(2):
            mine = slice(2 * half, 2 * half + 2)
            each(side.sends & (core == half), side.rates[mine], leave)
            each(side.receives & (core == half), side.forward[mine], leave)
    for copy in up_early + up_state:
        copy.wait_send()


def body(adjoint_iterate, innovations, station_cells, diffusivity, wind_x, wind_y, vertical_mixing):
    field = (LEV, TX, NY)
    f32, i32 = jnp.float32, jnp.int32
    scratch = (
        [pltpu.VMEM((STEPS_DEV,) + field, f32)] * 3
        + [pltpu.VMEM((STEPS_DEV + 4, LEV, NY), f32)] * 3
        + [pltpu.VMEM((STEPS_DEV, NY), i32)] * 6
        + [pltpu.VMEM((4,) + field, f32)] * 3
        + [pltpu.VMEM((LEV, 2, 6, TX, NY), f32)]
        + [pltpu.VMEM((STEPS_DEV + 4, LEV, 2, TX, NY), f32)]
        + [pltpu.VMEM((GROUP, LEV, 2, TX, NY), f32)] * 2
        + [pltpu.VMEM((OWN,) + field, f32)]
        + [pltpu.SemaphoreType.DMA((TRANSFERS,))] * 2
        + [pltpu.SemaphoreType.DMA((7,)), pltpu.SemaphoreType.REGULAR]
    )
    return pl.pallas_call(
        functools.partial(kernel, lax.axis_size("tm"), lax.axis_size("space")),
        out_shape=jax.ShapeDtypeStruct((STEPS_DEV,) + field, f32),
        in_specs=[pl.BlockSpec(memory_space=pl.ANY)] * 7,
        out_specs=pl.BlockSpec(memory_space=pltpu.VMEM),
        scratch_shapes=scratch,
        compiler_params=pltpu.CompilerParams(
            collective_id=0, has_side_effects=True, vmem_limit_bytes=24 * 2**20
        ),
        name="update",
    )(*[
        pltpu.with_memory_space_constraint(x, pltpu.HBM)
        for x in (adjoint_iterate, innovations, station_cells, diffusivity, wind_x, wind_y, vertical_mixing)
    ])


def solution(mesh):
    in_specs = (
        P("tm", None, "space", None),
        P("tm", None, "space"),
        P("tm", "space"),
        P(None, "space", None),
        P(None, "space", None),
        P(None, "space", None),
        P(None, "space", None),
    )
    out_specs = P("tm", None, "space", None)
    return jax.shard_map(body, mesh=mesh, in_specs=in_specs, out_specs=out_specs, check_vma=False)
```
